32 devices in a mesh: dp: 8 (over z, core), ctx: 4 (over y, x).
Axes of the slice: x: 2, y: 2, z: 4, core: 2. Of those that a mesh axis runs over, the one named last changes fastest.
Arguments:
- inputs: bfloat16 [32, 1024, 576], P('dp', 'ctx'), may hold values from -6 to 6
- bounds: int32 [32, 2], P('dp'), may hold values from 1 to 1023, as said below
- span_order: int32 [8], replicated, may hold values from 0 to 7, each once
- attn_gain: bfloat16 [576], P('dp'), may hold values from 0.5 to 1.5
- w_query: bfloat16 [576, 576], P('dp', 'ctx'), may hold values from -0.25 to 0.25
- w_key: bfloat16 [576, 192], P('dp', 'ctx'), may hold values from -0.25 to 0.25
- w_value: bfloat16 [576, 192], P('dp', 'ctx'), may hold values from -0.25 to 0.25
- w_out: bfloat16 [576, 576], P('dp', 'ctx'), may hold values from -4 to 4
- ffn_gain: bfloat16 [576], P('dp'), may hold values from 0.5 to 1.5
- w_gate: bfloat16 [576, 1536], P('dp', 'ctx'), may hold values from -0.25 to 0.25
- w_up: bfloat16 [576, 1536], P('dp', 'ctx'), may hold values from -0.25 to 0.25
- w_down: bfloat16 [1536, 576], P('dp', 'ctx'), may hold values from -0.15625 to 0.15625
- cotangent: bfloat16 [32, 1024, 576], P('dp', 'ctx'), may hold values from -6 to 6
Outputs:
- output: bfloat16 [32, 1024, 576], P('dp', 'ctx')
- input_grad: bfloat16 [32, 1024, 576], P('dp', 'ctx')
- attn_gain_grad: float32 [576], P('dp')
- query_grad: float32 [576, 576], P('dp', 'ctx')
- key_grad: float32 [576, 192], P('dp', 'ctx')
- value_grad: float32 [576, 192], P('dp', 'ctx')
- out_grad: float32 [576, 576], P('dp', 'ctx')
- ffn_gain_grad: float32 [576], P('dp')
- gate_grad: float32 [576, 1536], P('dp', 'ctx')
- up_grad: float32 [576, 1536], P('dp', 'ctx')
- down_grad: float32 [1536, 576], P('dp', 'ctx')
The draws below stay inside these ranges and needn't reach their ends.
Inputs may be any that keep to these rules, and one draw needn't show every extreme that they name: Sequence s holds the documents [0, bounds[s,0]), [bounds[s,0], bounds[s,1]) and [bounds[s,1], 1024) of positions; bounds[s,0] < 128 and bounds[s,1] > 896. A permutation: layout slot j (tokens j * 128 to (j + 1) * 128 - 1 along a sequence) holds the sequence's span span_order[j].
All inputs are finite; a program needn't handle non-finite values.
Results may differ from the reference program's by a relative error of at most 0.024.
Values may be sent and summed in bfloat16 or wider, within the bound.
No kernel may reach another device: no remote copies, remote signals or barrier semaphores. Data moves between devices by JAX's collectives and lax.ppermute only.
A program may use at most 320 MiB of HBM per device.

```python
import math
import jax
import jax.numpy as jnp
from jax import lax

D = 576
HEADS = 9
KV_HEADS = 3
HEAD_DIM = 64
FF = 1536
BLK = 128
NCHUNK = 8
LEN = 1024
SEQS = 32


def draw_bounds(key, part):
    key = jax.random.fold_in(key, 11)
    early_key, late_key = jax.random.split(key)
    early_end = jax.random.randint(early_key, (SEQS,), 1, BLK)
    late_start = jax.random.randint(late_key, (SEQS,), LEN - BLK + 1, LEN)
    return jnp.stack([early_end, late_start], axis=1).astype(jnp.int32)


def block_levels(own_key, extent, cuts, least, top_value):
    factor_of, own = 1.0, jax.random.fold_in(own_key, 6)
    for dim, parts in cuts:
        steps = jnp.exp(jax.random.uniform(jax.random.fold_in(own, dim), (parts,), jnp.float32, least / len(cuts), top_value / len(cuts)))
        factor_of = factor_of * jnp.repeat(steps, extent[dim] // parts).reshape([-1 if axis == dim else 1 for axis in range(len(extent))])
    return factor_of


def gaussian(rng, dims, scale, limit, shards=(), held_as=jnp.bfloat16):
    drawn = jax.random.normal(rng, dims, jnp.float32) * scale
    if len(shards) > 0:
        drawn = block_levels(rng, dims, shards, -0.22, 0.18) * drawn
    return jnp.clip(drawn, min=-limit, max=limit).astype(held_as)


def setup_inputs(seed: int = 0) -> dict:
    keys = jax.random.split(jax.random.key(seed), 14)
    return {
        "inputs": gaussian(keys[0], (SEQS, LEN, D), 1.0, 6.0, ((0, 8), (1, 4))),
        "bounds": draw_bounds(jax.random.fold_in(keys[13], 71), 0),
        "span_order": jax.random.permutation(keys[2], NCHUNK).astype(jnp.int32),
        "attn_gain": jnp.clip(1.0 + 0.1 * jax.random.normal(keys[3], (D,), jnp.float32), 0.5, 1.5).astype(jnp.bfloat16),
        "w_query": gaussian(keys[4], (D, D), D ** -0.5, 0.25, ((0, 8), (1, 4))),
        "w_key": gaussian(keys[5], (D, KV_HEADS * HEAD_DIM), D ** -0.5, 0.25, ((0, 8), (1, 4))),
        "w_value": gaussian(keys[6], (D, KV_HEADS * HEAD_DIM), D ** -0.5, 0.25, ((0, 8), (1, 4))),
        "w_out": gaussian(keys[7], (D, D), (max(1, 4 * D // LEN)) ** -0.5, 4.0, ((0, 8), (1, 4))),
        "ffn_gain": jnp.clip(1.0 + 0.1 * jax.random.normal(keys[8], (D,), jnp.float32), 0.5, 1.5).astype(jnp.bfloat16),
        "w_gate": gaussian(keys[9], (D, FF), D ** -0.5, 0.25, ((0, 8), (1, 4))),
        "w_up": gaussian(keys[10], (D, FF), D ** -0.5, 0.25, ((0, 8), (1, 4))),
        "w_down": gaussian(keys[11], (FF, D), FF ** -0.5, 0.15625, ((0, 8), (1, 4))),
        "cotangent": gaussian(keys[12], (SEQS, LEN, D), 1.0, 6.0, ((0, 8), (1, 4))),
    }


EPSILON = 1e-05
THETA = 100000.0
NEG_LARGE = -1e+30

@jax.custom_vjp
def low(v):
    return lax.optimization_barrier(v.astype(jnp.bfloat16)).astype(jnp.float32)

@jax.custom_vjp
def low_back(v):
    return v

def low_keep(v):
    return (low(v), None)

def low_pass(kept, grad):
    return (grad,)

def back_keep(v):
    return (v, None)

def back_low(kept, grad):
    return (low(grad),)
low.defvjp(low_keep, low_pass)
low_back.defvjp(back_keep, back_low)

def rotary_tables(positions):
    half_dim = HEAD_DIM // 2
    frequency = THETA ** (-jnp.arange(half_dim).astype(jnp.float32) / half_dim)
    angles = positions.astype(jnp.float32)[:, None] * frequency[None, :]
    return (jnp.cos(angles)[:, None, :], jnp.sin(angles)[:, None, :])

def rotate(values_in, cosine, sine):
    half_dim = HEAD_DIM // 2
    first_half = values_in[..., :half_dim]
    second_half = values_in[..., half_dim:]
    return jnp.concatenate([first_half * cosine - second_half * sine, second_half * cosine + first_half * sine], axis=-1)

def rms_scale(values_in, gain_vec):
    return values_in * lax.rsqrt(lax.optimization_barrier(jnp.mean(values_in * values_in, axis=-1, keepdims=True)) + EPSILON) * gain_vec

def layer(token_embeddings, positions, segment, weights):
    attn_gain, w_query, w_key, w_value, w_out, ffn_gain, w_gate, w_up, w_down = weights
    highest = lax.Precision.HIGHEST
    length = token_embeddings.shape[0]
    group = HEADS // KV_HEADS
    score_scale = HEAD_DIM ** (-0.5)
    normed = low(rms_scale(token_embeddings, attn_gain))
    query_pre = low_back(jnp.dot(normed, w_query, precision=highest))
    key_pre = low_back(jnp.dot(normed, w_key, precision=highest))
    value_rows = low(low_back(jnp.dot(normed, w_value, precision=highest))).reshape(length, KV_HEADS, HEAD_DIM)
    cosine, sine = rotary_tables(positions)
    query_rows = low(rotate(query_pre.reshape(length, HEADS, HEAD_DIM), cosine, sine))
    key_rows = low(rotate(key_pre.reshape(length, KV_HEADS, HEAD_DIM), cosine, sine))
    block_rows = math.gcd(length, 512)
    block_count = length // block_rows
    query_blocks = query_rows.reshape(block_count, block_rows, KV_HEADS, group, HEAD_DIM)
    pos_blocks = positions.reshape(block_count, block_rows)
    seg_blocks = segment.reshape(block_count, block_rows)

    def attend(block_item):
        rows_query, rows_pos, rows_seg = block_item
        scores = low_back(score_scale * jnp.einsum('tgrd,kgd->tgrk', rows_query, key_rows, precision=highest))
        allowed = (positions[None, :] <= rows_pos[:, None]) & (segment[None, :] == rows_seg[:, None])
        scores = jnp.where(allowed[:, None, None, :], scores, NEG_LARGE)
        row_max = lax.optimization_barrier(jnp.max(scores, axis=-1, keepdims=True))
        exp_scores = jnp.exp(scores - row_max)
        attention = low(exp_scores / lax.optimization_barrier(jnp.sum(exp_scores, axis=-1, keepdims=True)))
        return jnp.einsum('tgrk,kgd->tgrd', attention, value_rows, precision=highest)
    mixture = lax.map(jax.checkpoint(attend), (query_blocks, pos_blocks, seg_blocks))
    mixture = low(low_back(mixture.reshape(length, HEADS * HEAD_DIM)))
    hidden_residual = token_embeddings + low_back(jnp.dot(mixture, w_out, precision=highest))
    normed_ffn = low(rms_scale(hidden_residual, ffn_gain))
    gate_value = low_back(jnp.dot(normed_ffn, w_gate, precision=highest))
    up_value = low_back(jnp.dot(normed_ffn, w_up, precision=highest))
    inner_act = low(gate_value * jax.nn.sigmoid(gate_value) * up_value)
    return hidden_residual + low_back(jnp.dot(inner_act, w_down, precision=highest))

def reference(inputs, bounds, span_order, attn_gain, w_query, w_key, w_value, w_out, ffn_gain, w_gate, w_up, w_down, cotangent):
    length = inputs.shape[1]
    block_len = length // span_order.shape[0]
    offsets = jnp.arange(length).astype(jnp.int32)
    positions = (span_order[offsets // block_len] * block_len + offsets % block_len).astype(jnp.int32)
    params = (attn_gain.astype(jnp.float32), w_query.astype(jnp.float32), w_key.astype(jnp.float32), w_value.astype(jnp.float32), w_out.astype(jnp.float32), ffn_gain.astype(jnp.float32), w_gate.astype(jnp.float32), w_up.astype(jnp.float32), w_down.astype(jnp.float32))

    def one_sequence(totals, seq_item):
        token_embeddings, limits, tangent = seq_item
        segment = (positions >= limits[0]).astype(jnp.int32) + (positions >= limits[1]).astype(jnp.int32)

        def forward(tokens_in, weights):
            return layer(tokens_in, positions, segment, weights)
        result, pullback = jax.vjp(forward, token_embeddings.astype(jnp.float32), params)
        grad_in, grad_weights = pullback(tangent.astype(jnp.float32))
        totals = jax.tree.map(lambda left, right: left + right, totals, grad_weights)
        return (totals, (result.astype(jnp.bfloat16), grad_in.astype(jnp.bfloat16)))
    zeros_init = tuple((jnp.zeros_like(weight) for weight in params))
    totals, (outputs, grads) = lax.scan(one_sequence, zeros_init, (inputs, bounds, cotangent))
    return (outputs, grads, totals[0], totals[1], totals[2], totals[3], totals[4], totals[5], totals[6], totals[7], totals[8])
```

```python
import jax
import jax.numpy as jnp
from jax import lax
from jax.experimental import pallas as pl
from jax.experimental.pallas import tpu as pltpu
from jax.sharding import PartitionSpec as P

HEADS = 9
KV_HEADS = 3
HEAD_DIM = 64
FF = 1536
MICRO = 2


EPSILON = 1e-05
THETA = 100000.0
NEG_LARGE = -1e30


def rotary_tables(positions):
    half_dim = HEAD_DIM // 2
    frequency = THETA ** (-jnp.arange(half_dim).astype(jnp.float32) / half_dim)
    angles = positions.astype(jnp.float32)[:, None] * frequency[None, :]
    return (jnp.cos(angles)[None, :, None, :], jnp.sin(angles)[None, :, None, :])


def rotate(values_in, cosine, sine):
    half_dim = HEAD_DIM // 2
    first_half = values_in[..., :half_dim]
    second_half = values_in[..., half_dim:]
    return jnp.concatenate(
        [first_half * cosine - second_half * sine, second_half * cosine + first_half * sine],
        axis=-1,
    )


def rotate_back(grads_in, cosine, sine):
    half_dim = HEAD_DIM // 2
    first_half = grads_in[..., :half_dim]
    second_half = grads_in[..., half_dim:]
    return jnp.concatenate(
        [first_half * cosine + second_half * sine, second_half * cosine - first_half * sine],
        axis=-1,
    )


def positions_of(start, count, span_order, block_len):
    offsets = start + jnp.arange(count, dtype=jnp.int32)
    slots = offsets // block_len
    table = jnp.arange(span_order.shape[0], dtype=jnp.int32)
    chosen = jnp.sum(jnp.where(slots[:, None] == table[None, :], span_order[None, :], 0), axis=1)
    return chosen * block_len + offsets % block_len


def segments_of(positions, limits):
    return (positions[None, :] >= limits[:, 0:1]).astype(jnp.int32) + (
        positions[None, :] >= limits[:, 1:2]
    ).astype(jnp.int32)


def root_mean_square_pieces(values_in):
    inv_root = lax.rsqrt(jnp.mean(values_in * values_in, axis=-1, keepdims=True) + EPSILON)
    return (values_in * inv_root, inv_root)


def root_mean_square_backward(grad_hat, normal_hat, inv_root):
    return inv_root * (
        grad_hat - normal_hat * jnp.mean(grad_hat * normal_hat, axis=-1, keepdims=True)
    )


def key_mask(query_pos, query_seg, key_pos, key_seg):
    allowed = (key_pos[None, None, :] <= query_pos[None, :, None]) & (
        key_seg[:, None, :] == query_seg[:, :, None]
    )
    return allowed[:, :, None, None, :]


def attend_piece(
    carry,
    piece,
    start,
    query_rows,
    query_pos,
    query_seg,
    limits,
    span_order,
    block_len,
    score_scale,
):
    run_max, run_sum, run_acc = carry
    key_piece, value_piece = piece
    seqs_here = key_piece.shape[0]
    count = key_piece.shape[1]
    key_pos = positions_of(start, count, span_order, block_len)
    key_seg = segments_of(key_pos, limits)
    allowed = key_mask(query_pos, query_seg, key_pos, key_seg)
    keys_four = key_piece.reshape(seqs_here, count, KV_HEADS, HEAD_DIM)
    values_four = value_piece.reshape(seqs_here, count, KV_HEADS, HEAD_DIM)
    scores = (
        jnp.einsum("stgrd,skgd->stgrk", query_rows, keys_four, preferred_element_type=jnp.float32)
        * score_scale
    )
    new_max = jnp.maximum(run_max, jnp.max(jnp.where(allowed, scores, NEG_LARGE), axis=-1))
    weights_exp = jnp.where(allowed, jnp.exp(scores - new_max[..., None]), 0.0)
    run_sum = jnp.sum(weights_exp, axis=-1)
    run_acc = jnp.einsum(
        "stgrk,skgd->stgrd",
        weights_exp.astype(jnp.bfloat16),
        values_four,
        preferred_element_type=jnp.float32,
    )
    return (new_max, run_sum, run_acc)


def general_shards(
    inputs,
    bounds,
    span_order,
    attn_gain,
    w_query,
    w_key,
    w_value,
    w_out,
    ffn_gain,
    w_gate,
    w_up,
    w_down,
    cotangent,
):
    seq_local = inputs.shape[0]
    rows = inputs.shape[1]
    width = inputs.shape[2]
    kv_width = KV_HEADS * HEAD_DIM
    group = HEADS // KV_HEADS
    block_len = rows // 2
    micro_seqs = seq_local // MICRO
    ctx_index = lax.axis_index("ctx")
    score_scale = HEAD_DIM ** (-0.5)
    my_start = ctx_index * rows
    positions = positions_of(my_start, rows, span_order, block_len)
    cosine, sine = rotary_tables(positions)

    def fetch():
        columns = (
            lax.all_gather(w_query, "ctx", axis=1, tiled=True),
            lax.all_gather(w_key, "ctx", axis=1, tiled=True),
            lax.all_gather(w_value, "ctx", axis=1, tiled=True),
            lax.all_gather(w_out, "ctx", axis=1, tiled=True),
            lax.all_gather(w_gate, "ctx", axis=1, tiled=True),
            lax.all_gather(w_up, "ctx", axis=1, tiled=True),
            lax.all_gather(w_down, "ctx", axis=1, tiled=True),
        )
        return (
            lax.all_gather(columns[0], "dp", axis=0, tiled=True),
            lax.all_gather(columns[1], "dp", axis=0, tiled=True),
            lax.all_gather(columns[2], "dp", axis=0, tiled=True),
            lax.all_gather(columns[3], "dp", axis=0, tiled=True),
            lax.all_gather(columns[4], "dp", axis=0, tiled=True),
            lax.all_gather(columns[5], "dp", axis=0, tiled=True),
            lax.all_gather(columns[6], "dp", axis=0, tiled=True),
            lax.all_gather(attn_gain, "dp", axis=0, tiled=True),
            lax.all_gather(ffn_gain, "dp", axis=0, tiled=True),
        )

    tot_query = jnp.zeros((width, width), jnp.float32)
    tot_key = jnp.zeros((width, kv_width), jnp.float32)
    tot_value = jnp.zeros((width, kv_width), jnp.float32)
    tot_out = jnp.zeros((width, width), jnp.float32)
    tot_gate = jnp.zeros((width, FF), jnp.float32)
    tot_up = jnp.zeros((width, FF), jnp.float32)
    tot_down = jnp.zeros((FF, width), jnp.float32)
    attention_gain_gradient_total = jnp.zeros((width,), jnp.float32)
    feedforward_gain_gradient_total = jnp.zeros((width,), jnp.float32)
    outputs_list = []
    grads_list = []
    for micro in range(MICRO):
        weights = fetch()
        mat_query, mat_key, mat_value, mat_out, mat_gate, mat_up, mat_down = weights[:7]
        attention_norm_gain = weights[7].astype(jnp.float32)
        feedforward_norm_gain = weights[8].astype(jnp.float32)
        first_seq = micro * micro_seqs
        token_embeddings = inputs[first_seq : first_seq + micro_seqs].astype(jnp.float32)
        limits = bounds[first_seq : first_seq + micro_seqs]
        query_seg = segments_of(positions, limits)
        attention_unit_rows, attention_inverse_root = root_mean_square_pieces(token_embeddings)
        attention_normed_input = (attention_unit_rows * attention_norm_gain).astype(jnp.bfloat16)
        query_pre = jnp.dot(attention_normed_input, mat_query, preferred_element_type=jnp.float32)
        key_pre = jnp.dot(attention_normed_input, mat_key, preferred_element_type=jnp.float32)
        value_rows = jnp.dot(
            attention_normed_input, mat_value, preferred_element_type=jnp.float32
        ).astype(jnp.bfloat16)
        query_rows = rotate(
            query_pre.reshape(micro_seqs, rows, HEADS, HEAD_DIM), cosine, sine
        ).astype(jnp.bfloat16)
        query_rows = query_rows.reshape(micro_seqs, rows, KV_HEADS, group, HEAD_DIM)
        key_rows = rotate(
            key_pre.reshape(micro_seqs, rows, KV_HEADS, HEAD_DIM), cosine, sine
        ).astype(jnp.bfloat16)
        key_rows = key_rows.reshape(micro_seqs, rows, kv_width)
        init_state = (
            jnp.full((micro_seqs, rows, KV_HEADS, group), NEG_LARGE, jnp.float32),
            jnp.zeros((micro_seqs, rows, KV_HEADS, group), jnp.float32),
            jnp.zeros((micro_seqs, rows, KV_HEADS, group, HEAD_DIM), jnp.float32),
        )
        run_max, run_sum, run_acc = attend_piece(
            init_state,
            (
                lax.all_gather(key_rows, "ctx", axis=1, tiled=True),
                lax.all_gather(value_rows, "ctx", axis=1, tiled=True),
            ),
            jnp.int32(0),
            query_rows,
            positions,
            query_seg,
            limits,
            span_order,
            block_len,
            score_scale,
        )
        mixture = run_acc / run_sum[..., None]
        log_total = run_max + jnp.log(run_sum)
        mixture_low = mixture.reshape(micro_seqs, rows, width).astype(jnp.bfloat16)
        hidden_residual = token_embeddings + jnp.dot(
            mixture_low, mat_out, preferred_element_type=jnp.float32
        )
        feedforward_unit_rows, feedforward_inverse_root = root_mean_square_pieces(hidden_residual)
        feedforward_normed_input = (feedforward_unit_rows * feedforward_norm_gain).astype(
            jnp.bfloat16
        )
        gate_value = jnp.dot(feedforward_normed_input, mat_gate, preferred_element_type=jnp.float32)
        up_value = jnp.dot(feedforward_normed_input, mat_up, preferred_element_type=jnp.float32)
        sigmoid_gate = jax.nn.sigmoid(gate_value)
        silu_gate = gate_value * sigmoid_gate
        inner_act = (silu_gate * up_value).astype(jnp.bfloat16)
        result = hidden_residual + jnp.dot(inner_act, mat_down, preferred_element_type=jnp.float32)
        outputs_list.append(result.astype(jnp.bfloat16))
        weights = fetch()
        mat_query, mat_key, mat_value, mat_out, mat_gate, mat_up, mat_down = weights[:7]
        output_gradient_float = cotangent[first_seq : first_seq + micro_seqs].astype(jnp.float32)
        grad_ffn_low = output_gradient_float.astype(jnp.bfloat16)
        tot_down = tot_down + jnp.einsum(
            "stf,std->fd", inner_act, grad_ffn_low, preferred_element_type=jnp.float32
        )
        grad_inner = jnp.einsum(
            "std,fd->stf", grad_ffn_low, mat_down, preferred_element_type=jnp.float32
        )
        grad_gate = (
            grad_inner * up_value * sigmoid_gate * (1.0 + gate_value * (1.0 - sigmoid_gate))
        ).astype(jnp.bfloat16)
        grad_up = (grad_inner * silu_gate).astype(jnp.bfloat16)
        tot_gate = tot_gate + jnp.einsum(
            "ste,stf->ef", feedforward_normed_input, grad_gate, preferred_element_type=jnp.float32
        )
        tot_up = tot_up + jnp.einsum(
            "ste,stf->ef", feedforward_normed_input, grad_up, preferred_element_type=jnp.float32
        )
        feedforward_normed_gradient = jnp.einsum(
            "stf,ef->ste", grad_gate, mat_gate, preferred_element_type=jnp.float32
        ) + jnp.einsum("stf,ef->ste", grad_up, mat_up, preferred_element_type=jnp.float32)
        feedforward_gain_gradient_total = feedforward_gain_gradient_total + jnp.sum(
            feedforward_normed_gradient * feedforward_unit_rows, axis=(0, 1)
        )
        hidden_state_gradient = output_gradient_float + root_mean_square_backward(
            feedforward_normed_gradient * feedforward_norm_gain,
            feedforward_unit_rows,
            feedforward_inverse_root,
        )
        grad_attn_low = hidden_state_gradient.astype(jnp.bfloat16)
        tot_out = tot_out + jnp.einsum(
            "std,ste->de", mixture_low, grad_attn_low, preferred_element_type=jnp.float32
        )
        grad_mix_low = jnp.einsum(
            "ste,de->std", grad_attn_low, mat_out, preferred_element_type=jnp.float32
        ).astype(jnp.bfloat16)
        grad_mix_five = grad_mix_low.reshape(micro_seqs, rows, KV_HEADS, group, HEAD_DIM)
        delta_rows = jnp.sum(grad_mix_five.astype(jnp.float32) * mixture, axis=-1)

        def back_piece(key_piece, value_piece, start):
            key_pos = positions_of(start, rows, span_order, block_len)
            key_seg = segments_of(key_pos, limits)
            allowed = key_mask(positions, query_seg, key_pos, key_seg)
            keys_four = key_piece.reshape(micro_seqs, rows, KV_HEADS, HEAD_DIM)
            values_four = value_piece.reshape(micro_seqs, rows, KV_HEADS, HEAD_DIM)
            scores = (
                jnp.einsum(
                    "stgrd,skgd->stgrk", query_rows, keys_four, preferred_element_type=jnp.float32
                )
                * score_scale
            )
            probs = jnp.where(allowed, jnp.exp(scores - log_total[..., None]), 0.0)
            grad_prob = jnp.einsum(
                "stgrd,skgd->stgrk", grad_mix_five, values_four, preferred_element_type=jnp.float32
            )
            grad_score = (probs * (grad_prob - delta_rows[..., None])).astype(jnp.bfloat16)
            query_term = jnp.einsum(
                "stgrk,skgd->stgrd", grad_score, keys_four, preferred_element_type=jnp.float32
            )
            key_term = jnp.einsum(
                "stgrk,stgrd->skgd", grad_score, query_rows, preferred_element_type=jnp.float32
            )
            value_term = jnp.einsum(
                "stgrk,stgrd->skgd",
                probs.astype(jnp.bfloat16),
                grad_mix_five,
                preferred_element_type=jnp.float32,
            )
            return (
                query_term,
                key_term.reshape(micro_seqs, rows, kv_width),
                value_term.reshape(micro_seqs, rows, kv_width),
            )

        query_zero = jnp.zeros((micro_seqs, rows, KV_HEADS, group, HEAD_DIM), jnp.float32)
        key_source = (
            lax.all_gather(key_rows, "ctx", axis=1, tiled=True),
            lax.all_gather(value_rows, "ctx", axis=1, tiled=True),
        )
        source_keys, source_values = key_source
        full_len = source_keys.shape[1]

        def backward_step(position_index, state):
            grad_query, key_sums, value_sums = state
            start = position_index * rows
            key_piece = lax.dynamic_slice_in_dim(source_keys, start, rows, 1)
            value_piece = lax.dynamic_slice_in_dim(source_values, start, rows, 1)
            query_term, key_term, value_term = back_piece(key_piece, value_piece, start)
            key_sums = lax.dynamic_update_slice_in_dim(key_sums, key_term, start, 1)
            value_sums = lax.dynamic_update_slice_in_dim(value_sums, value_term, start, 1)
            return (grad_query + query_term, key_sums, value_sums)

        back_init = (
            query_zero,
            jnp.zeros((micro_seqs, full_len, kv_width), jnp.float32),
            jnp.zeros((micro_seqs, full_len, kv_width), jnp.float32),
        )
        grad_query, key_sums, value_sums = lax.fori_loop(
            0, full_len // rows, backward_step, back_init
        )
        key_mine, value_mine = (
            lax.psum_scatter(
                key_sums.astype(jnp.bfloat16), "ctx", scatter_dimension=1, tiled=True
            ).astype(jnp.float32),
            lax.psum_scatter(
                value_sums.astype(jnp.bfloat16), "ctx", scatter_dimension=1, tiled=True
            ).astype(jnp.float32),
        )
        grad_q_low = rotate_back(
            (grad_query * score_scale).reshape(micro_seqs, rows, HEADS, HEAD_DIM), cosine, sine
        )
        grad_q_low = grad_q_low.reshape(micro_seqs, rows, width).astype(jnp.bfloat16)
        grad_k_low = rotate_back(
            (key_mine * score_scale).reshape(micro_seqs, rows, KV_HEADS, HEAD_DIM), cosine, sine
        )
        grad_k_low = grad_k_low.reshape(micro_seqs, rows, kv_width).astype(jnp.bfloat16)
        grad_v_low = value_mine.astype(jnp.bfloat16)
        tot_query = tot_query + jnp.einsum(
            "ste,std->ed", attention_normed_input, grad_q_low, preferred_element_type=jnp.float32
        )
        tot_key = tot_key + jnp.einsum(
            "ste,std->ed", attention_normed_input, grad_k_low, preferred_element_type=jnp.float32
        )
        tot_value = tot_value + jnp.einsum(
            "ste,std->ed", attention_normed_input, grad_v_low, preferred_element_type=jnp.float32
        )
        attention_normed_gradient = (
            jnp.einsum("std,ed->ste", grad_q_low, mat_query, preferred_element_type=jnp.float32)
            + jnp.einsum("std,ed->ste", grad_k_low, mat_key, preferred_element_type=jnp.float32)
            + jnp.einsum("std,ed->ste", grad_v_low, mat_value, preferred_element_type=jnp.float32)
        )
        attention_gain_gradient_total = attention_gain_gradient_total + jnp.sum(
            attention_normed_gradient * attention_unit_rows, axis=(0, 1)
        )
        layer_input_gradient = hidden_state_gradient + root_mean_square_backward(
            attention_normed_gradient * attention_norm_gain,
            attention_unit_rows,
            attention_inverse_root,
        )
        grads_list.append(layer_input_gradient.astype(jnp.bfloat16))
    row_sums = (
        lax.psum_scatter(
            tot_query.astype(jnp.bfloat16), "dp", scatter_dimension=0, tiled=True
        ).astype(jnp.float32),
        lax.psum_scatter(
            tot_key.astype(jnp.bfloat16), "dp", scatter_dimension=0, tiled=True
        ).astype(jnp.float32),
        lax.psum_scatter(
            tot_value.astype(jnp.bfloat16), "dp", scatter_dimension=0, tiled=True
        ).astype(jnp.float32),
        lax.psum_scatter(
            tot_out.astype(jnp.bfloat16), "dp", scatter_dimension=0, tiled=True
        ).astype(jnp.float32),
        lax.psum_scatter(
            tot_gate.astype(jnp.bfloat16), "dp", scatter_dimension=0, tiled=True
        ).astype(jnp.float32),
        lax.psum_scatter(tot_up.astype(jnp.bfloat16), "dp", scatter_dimension=0, tiled=True).astype(
            jnp.float32
        ),
        lax.psum_scatter(
            tot_down.astype(jnp.bfloat16), "dp", scatter_dimension=0, tiled=True
        ).astype(jnp.float32),
        lax.psum_scatter(
            attention_gain_gradient_total.astype(jnp.bfloat16),
            "dp",
            scatter_dimension=0,
            tiled=True,
        ).astype(jnp.float32),
        lax.psum_scatter(
            feedforward_gain_gradient_total.astype(jnp.bfloat16),
            "dp",
            scatter_dimension=0,
            tiled=True,
        ).astype(jnp.float32),
    )
    col_sums = (
        lax.psum_scatter(
            row_sums[0].astype(jnp.bfloat16), "ctx", scatter_dimension=1, tiled=True
        ).astype(jnp.float32),
        lax.psum_scatter(
            row_sums[1].astype(jnp.bfloat16), "ctx", scatter_dimension=1, tiled=True
        ).astype(jnp.float32),
        lax.psum_scatter(
            row_sums[2].astype(jnp.bfloat16), "ctx", scatter_dimension=1, tiled=True
        ).astype(jnp.float32),
        lax.psum_scatter(
            row_sums[3].astype(jnp.bfloat16), "ctx", scatter_dimension=1, tiled=True
        ).astype(jnp.float32),
        lax.psum_scatter(
            row_sums[4].astype(jnp.bfloat16), "ctx", scatter_dimension=1, tiled=True
        ).astype(jnp.float32),
        lax.psum_scatter(
            row_sums[5].astype(jnp.bfloat16), "ctx", scatter_dimension=1, tiled=True
        ).astype(jnp.float32),
        lax.psum_scatter(
            row_sums[6].astype(jnp.bfloat16), "ctx", scatter_dimension=1, tiled=True
        ).astype(jnp.float32),
    )
    gain_totals = lax.psum((row_sums[7], row_sums[8]), "ctx")
    return (
        jnp.concatenate(outputs_list, axis=0),
        jnp.concatenate(grads_list, axis=0),
        gain_totals[0],
        col_sums[0],
        col_sums[1],
        col_sums[2],
        col_sums[3],
        gain_totals[1],
        col_sums[4],
        col_sums[5],
        col_sums[6],
    )


BF = jnp.bfloat16
F32 = jnp.float32
QB = 256
LOG2E = 1.4426950408889634
NN = (((1,), (0,)), ((), ()))
NT = (((1,), (1,)), ((), ()))
TN = (((0,), (0,)), ((), ()))
VMEM_LIMIT = 60 * 1024 * 1024


def dot(a, b, dims=NN):
    return lax.dot_general(a, b, dims, preferred_element_type=F32)


def call(body, outs, scratch, args, flops, name):
    specs = [pl.BlockSpec(memory_space=pltpu.SMEM)] + [
        pl.BlockSpec(memory_space=pltpu.VMEM) for _ in args[1:]
    ]
    moved = sum(a.size * a.dtype.itemsize for a in args)
    return pl.pallas_call(
        body,
        out_shape=outs,
        in_specs=specs,
        out_specs=[pl.BlockSpec(memory_space=pltpu.VMEM) for _ in outs],
        scratch_shapes=scratch,
        compiler_params=pltpu.CompilerParams(vmem_limit_bytes=VMEM_LIMIT),
        cost_estimate=pl.CostEstimate(flops=int(flops), bytes_accessed=moved, transcendentals=0),
        name=name,
    )(*args)


def shape(dims, dtype):
    return jax.ShapeDtypeStruct(dims, dtype)


def spans_in(info, dest, blocks):
    for r in range(4):
        dest[256 * r : 256 * r + 256, :] = blocks[r]


def span_rows(info, ref, p):
    start = pl.multiple_of(info[p] * 128, 128)
    return ref[pl.ds(start, 128), :]


def rotary_swap(v):
    lane = lax.broadcasted_iota(jnp.int32, v.shape, 1)
    return jnp.where(lane % 64 < 32, pltpu.roll(v, 96, 1), pltpu.roll(v, 32, 1))


def qkv_body(info, x_all, x1, x2, x3, *rest):
    pieces = rest[:8]
    cos_ref, sin_ref = rest[8:10]
    q_out, k_out, v_out, xp_out, n_out, wqk_out, wv_out, gain_out, raw, w32 = rest[10:]
    c, z, core = info[8], info[9], info[10]
    spans_in(info, raw, [x_all[c], x1[...], x2[...], x3[...]])
    for p in range(8):
        xp_out[128 * p : 128 * p + 128, :] = span_rows(info, raw, p)
    for j in range(2):
        for k in range(4):
            row = (lax.rem(z - k + 4, 4) * 2 + (core ^ j)) * 72
            row = pl.multiple_of(row, 8)
            for cc in range(4):
                w32[pl.ds(row, 72), 256 * cc : 256 * cc + 256] = pieces[4 * j + k][c ^ cc].astype(F32)
    wq = [w32[:, 256 * cc : 256 * cc + 144] for cc in range(4)]
    wk = [w32[:, 256 * cc + 144 : 256 * cc + 192] for cc in range(4)]
    wv = [w32[:, 256 * cc + 192 : 256 * cc + 240] for cc in range(4)]
    wqk_out[...] = jnp.concatenate(wq + wk, axis=1).astype(BF)
    wv_out[...] = jnp.concatenate(wv, axis=1).astype(BF)
    gains = jnp.transpose(w32[:, 128:256])
    gain_out[...] = gains[112:120, :]
    g1 = gains[112:113, :]
    for i in range(4):
        rows = pl.ds(256 * i, 256)
        x = xp_out[rows, :].astype(F32)
        inv = lax.rsqrt(jnp.mean(x * x, axis=-1, keepdims=True) + EPSILON)
        n = (x * inv * g1).astype(BF)
        n_out[rows, :] = n
        qk = dot(n, wqk_out[...])
        v = dot(n, wv_out[...])
        cs, sn = cos_ref[rows, :], sin_ref[rows, :]
        for b in range(6):
            t = qk[:, 128 * b : 128 * b + 128]
            t = (t * cs + rotary_swap(t) * sn).astype(BF)
            for u in range(2):
                h = 2 * b + u
                part = t[:, 64 * u : 64 * u + 64]
                if h < 9:
                    q_out[h // 3, i, 256 * (h % 3) : 256 * (h % 3) + 256, :] = part
                else:
                    k_out[h - 9, rows, :] = part
        v = v.astype(BF)
        for g in range(3):
            v_out[g, rows, :] = v[:, 64 * g : 64 * g + 64]


def segment_start(info, pos):
    b0, b1 = info[11], info[12]
    return jnp.where(pos >= b1, b1, jnp.where(pos >= b0, b0, 0))


def attend_body(info, q_ref, k_ref, v_ref, mix_out, lse_out, mix_scr, lse_scr):
    scale = 0.125 * LOG2E
    for i in range(4):
        n = 256 * (i + 1)
        kpos = lax.broadcasted_iota(jnp.int32, (256, 256), 1)
        qpos = lax.broadcasted_iota(jnp.int32, (256, 256), 0) + 256 * i
        first = segment_start(info, qpos)

        def head(h, carry, i=i, n=n, kpos=kpos, qpos=qpos, first=first):
            g, r = h // 3, h % 3
            q = q_ref[g, i, pl.ds(pl.multiple_of(r * 256, 256), 256), :]
            tiles = []
            top = None
            for j in range(i + 1):
                s = dot(q, k_ref[g, 256 * j : 256 * j + 256, :], NT) * scale
                ok = None
                if j == 0 or i == 3:
                    ok = (kpos + 256 * j) >= first
                if j == i:
                    causal = (kpos + 256 * j) <= qpos
                    ok = causal if ok is None else ok & causal
                if ok is not None:
                    s = jnp.where(ok, s, NEG_LARGE)
                tiles.append(s)
                m = jnp.maximum(s[:, :128], s[:, 128:])
                top = m if top is None else jnp.maximum(top, m)
            m = jnp.max(top, axis=-1, keepdims=True)
            total = None
            acc = None
            for j in range(i + 1):
                e = jnp.exp2(tiles[j] - m)
                part = e[:, :128] + e[:, 128:]
                total = part if total is None else total + part
                o = dot(e.astype(BF), v_ref[g, 256 * j : 256 * j + 256, :])
                acc = o if acc is None else acc + o
            total = jnp.sum(total, axis=-1, keepdims=True)
            mix_scr[h, 256 * i : 256 * i + 256, :] = (acc / total).astype(BF)
            lse = m + jnp.log2(total)
            lse_scr[h, :, 256 * i : 256 * i + 256] = jnp.transpose(jnp.broadcast_to(lse, (256, 128)))[0:8, :]
            return carry

        lax.fori_loop(0, 9, head, 0)
    mix_out[...] = jnp.concatenate([mix_scr[h] for h in range(9)], axis=1)
    lse_out[...] = lse_scr[...]


def ffn_body(info, xp, mix, gains, *rest):
    pieces = rest[:8]
    d_all, d1, d2, d3 = rest[8:12]
    y0, y1, y2, y3, dhid_out, dmix_out, delta_out, gm_out, go_out = rest[12:21]
    w32, o32, wg, wu, wd, wo, raw, normed, inner, dgate, dup, yscr, dattn, gsum = rest[21:]
    c, z, core = info[8], info[9], info[10]

    def collect(lane):
        for j in range(2):
            for r in range(4):
                col = pl.multiple_of(384 * (c ^ r), 128)
                for zz in range(4):
                    row = pl.multiple_of((2 * zz + (core ^ j)) * 72, 8)
                    k = lax.rem(z - zz + 4, 4)
                    w32[pl.ds(row, 72), pl.ds(col, 384)] = pieces[4 * j + r][k, :, lane : lane + 384].astype(F32)

    collect(0)
    wg[...] = w32[...].astype(BF)
    collect(384)
    wu[...] = w32[...].astype(BF)
    for r in range(4):
        for zz in range(4):
            k = lax.rem(z - zz + 4, 4)
            a = pieces[r][k, :, 768:1408].astype(F32)
            b = pieces[4 + r][k, :, 768:1408].astype(F32)
            lo = jnp.where(core == 0, a, b)
            hi = jnp.where(core == 0, b, a)
            for half in range(2):
                row = pl.multiple_of(144 * (c ^ r) + 72 * half, 8)
                w32[pl.ds(row, 72), 384 * zz : 384 * zz + 384] = jnp.concatenate(
                    [lo[:, 192 * half : 192 * half + 192], hi[:, 192 * half : 192 * half + 192]], axis=1
                )
            col = pl.multiple_of(256 * (c ^ r), 128)
            o32[144 * zz : 144 * zz + 72, pl.ds(col, 256)] = lo[:, 384:640]
            o32[144 * zz + 72 : 144 * zz + 144, pl.ds(col, 256)] = hi[:, 384:640]
    wd[...] = w32[...].astype(BF)
    wo[...] = jnp.concatenate([o32[:, 256 * cc : 256 * cc + 144] for cc in range(4)], axis=1).astype(BF)

    spans_in(info, raw, [d_all[c], d1[...], d2[...], d3[...]])
    g2 = gains[1:2, :]
    gsum[...] = jnp.zeros_like(gsum)

    def chunk(i, carry):
        rows = pl.ds(pl.multiple_of(256 * i, 256), 256)
        x = xp[rows, :].astype(F32)
        m = mix[rows, :]
        hidden = x + dot(m, wo[...])
        r2 = lax.rsqrt(jnp.mean(hidden * hidden, axis=-1, keepdims=True) + EPSILON)
        hat = hidden * r2
        n = (hat * g2).astype(BF)
        normed[rows, :] = n
        dlow = jnp.concatenate([span_rows(info, raw, 2 * i), span_rows(info, raw, 2 * i + 1)], axis=0)
        res = hidden
        dn = None
        for f in range(3):
            cols = slice(512 * f, 512 * f + 512)
            gate = dot(n, wg[:, cols])
            up = dot(n, wu[:, cols])
            sg = 1.0 / (1.0 + jnp.exp(-gate))
            silu = gate * sg
            act = (silu * up).astype(BF)
            inner[rows, cols] = act
            res = res + dot(act, wd[:, cols], NT)
            din = dot(dlow, wd[:, cols])
            dg = (din * up * (sg + silu * (1.0 - sg))).astype(BF)
            du = (din * silu).astype(BF)
            dgate[rows, cols] = dg
            dup[rows, cols] = du
            t = dot(dg, wg[:, cols], NT) + dot(du, wu[:, cols], NT)
            dn = t if dn is None else dn + t
        res = res.astype(BF)
        for u in range(2):
            start = pl.multiple_of(info[2 * i + u] * 128, 128)
            yscr[pl.ds(start, 128), :] = res[128 * u : 128 * u + 128, :]
        gsum[...] += jnp.sum((dn * hat).reshape(32, 8, 576), axis=0)
        e = dn * g2
        dh = dlow.astype(F32) + r2 * (e - hat * jnp.mean(e * hat, axis=-1, keepdims=True))
        dhid_out[rows, :] = dh
        da = dh.astype(BF)
        dattn[rows, :] = da
        dm = dot(da, wo[...], NT).astype(BF)
        prod = dm.astype(F32) * m.astype(F32)
        cols = []
        for h in range(9):
            part = dm[:, 64 * h : 64 * h + 64]
            dmix_out[h // 3, i, 256 * (h % 3) : 256 * (h % 3) + 256, :] = part
            cols.append(jnp.sum(prod[:, 64 * h : 64 * h + 64], axis=-1, keepdims=True))
        lane = lax.broadcasted_iota(jnp.int32, (256, 128), 1)
        table = jnp.zeros((256, 128), F32)
        for h in range(9):
            table = jnp.where(lane == h, cols[h], table)
        table = jnp.transpose(table)
        delta_out[i] = table[0:16, :]
        return carry

    lax.fori_loop(0, 4, chunk, 0)
    for r, y in enumerate((y0, y1, y2, y3)):
        y[...] = yscr[256 * r : 256 * r + 256, :]

    def deal(lane):
        for r in range(4):
            col = pl.multiple_of(384 * (c ^ r), 128)
            for k in range(4):
                zz = lax.rem(z + k, 4)
                for out, who in ((gm_out, core), (go_out, 1 - core)):
                    row = pl.multiple_of((2 * zz + who) * 72, 8)
                    out[r, k, :, lane : lane + 384] = w32[pl.ds(row, 72), pl.ds(col, 384)].astype(BF)

    w32[...] = dot(normed[...], dgate[...], TN)
    deal(0)
    w32[...] = dot(normed[...], dup[...], TN)
    deal(384)
    for i in range(8):
        start = pl.multiple_of(info[i] * 128, 128)
        normed[128 * i : 128 * i + 128, :] = raw[pl.ds(start, 128), :]
    w32[...] = dot(normed[...], inner[...], TN)
    og = dot(mix[...], dattn[...], TN)
    for cc in range(4):
        o32[:, 256 * cc : 256 * cc + 144] = og[:, 144 * cc : 144 * cc + 144]
    total = jnp.sum(gsum[...], axis=0, keepdims=True)
    gcol = jnp.transpose(jnp.broadcast_to(total, (128, 576)))
    for cc in range(4):
        o32[:, 256 * cc + 144 : 256 * cc + 256] = gcol[:, 0:112]
    for r in range(4):
        ocol = pl.multiple_of(256 * (c ^ r), 128)
        for k in range(4):
            zz = lax.rem(z + k, 4)
            dcol = pl.multiple_of(384 * zz, 128)
            a = w32[pl.ds(pl.multiple_of(144 * (c ^ r), 8), 72), pl.ds(dcol, 384)]
            b = w32[pl.ds(pl.multiple_of(144 * (c ^ r) + 72, 8), 72), pl.ds(dcol, 384)]
            left = [a[:, :192], b[:, :192]]
            right = [a[:, 192:], b[:, 192:]]
            for out, who in ((gm_out, core), (go_out, 1 - core)):
                row = pl.multiple_of((2 * zz + who) * 72, 8)
                o = o32[pl.ds(row, 72), pl.ds(ocol, 256)]
                d = [jnp.where(who == 0, u, v) for u, v in zip(left, right)]
                out[r, k, :, 768:1408] = jnp.concatenate(d + [o], axis=1).astype(BF)


def back_body(info, q_ref, k_ref, v_ref, dmix_ref, lse_ref, delta_ref, dq_out, dk_out, dv_out, dk_scr, dv_scr):
    scale = 0.125 * LOG2E

    def group(g, carry):
        dk_scr[...] = jnp.zeros_like(dk_scr)
        dv_scr[...] = jnp.zeros_like(dv_scr)
        for i in range(4):
            qpos = lax.broadcasted_iota(jnp.int32, (256, 256), 1) + 256 * i
            kpos = lax.broadcasted_iota(jnp.int32, (256, 256), 0)
            first = segment_start(info, qpos)
            for r in range(3):
                q = q_ref[g, i, 256 * r : 256 * r + 256, :]
                do = dmix_ref[g, i, 256 * r : 256 * r + 256, :]
                lse = lse_ref[3 * g + r, 0:1, 256 * i : 256 * i + 256]
                delta = delta_ref[i, pl.ds(3 * g + r, 1), :]
                dq = None
                for j in range(i + 1):
                    keys = slice(256 * j, 256 * j + 256)
                    kk = k_ref[g, keys, :]
                    s = dot(kk, q, NT) * scale
                    p = jnp.exp2(s - lse)
                    ok = None
                    if j == 0 or i == 3:
                        ok = (kpos + 256 * j) >= first
                    if j == i:
                        causal = (kpos + 256 * j) <= qpos
                        ok = causal if ok is None else ok & causal
                    if ok is not None:
                        p = jnp.where(ok, p, 0.0)
                    dp = dot(v_ref[g, keys, :], do, NT)
                    ds = (p * (dp - delta)).astype(BF)
                    dv_scr[keys, :] += dot(p.astype(BF), do)
                    dk_scr[keys, :] += dot(ds, q)
                    t = dot(ds, kk, TN)
                    dq = t if dq is None else dq + t
                dq_out[3 * g + r, 256 * i : 256 * i + 256, :] = dq
        dk_out[g] = dk_scr[...]
        dv_out[g] = dv_scr[...]
        return carry

    lax.fori_loop(0, 3, group, 0)


def tail_body(info, xp, n_ref, dq_ref, dk_ref, dv_ref, dhid, cos_ref, sin_ref, wqk, wv, gains, *rest):
    i0, i1, i2, i3, gm_out, go_out = rest[:6]
    yscr, dqk, dvl, gsum, w32 = rest[6:]
    c, z, core = info[8], info[9], info[10]
    g1 = gains[0:1, :]
    gsum[...] = jnp.zeros_like(gsum)
    for i in range(4):
        rows = pl.ds(256 * i, 256)
        cs, sn = cos_ref[rows, :], sin_ref[rows, :]
        for b in range(6):
            parts = []
            for u in range(2):
                h = 2 * b + u
                parts.append(dq_ref[h, rows, :] if h < 9 else dk_ref[h - 9, rows, :])
            t = jnp.concatenate(parts, axis=1) * 0.125
            dqk[rows, 128 * b : 128 * b + 128] = (t * cs - rotary_swap(t) * sn).astype(BF)
        dvl[rows, :] = jnp.concatenate([dv_ref[g, rows, :] for g in range(3)], axis=1).astype(BF)
        dn = dot(dqk[rows, :], wqk[...], NT) + dot(dvl[rows, :], wv[...], NT)
        x = xp[rows, :].astype(F32)
        r1 = lax.rsqrt(jnp.mean(x * x, axis=-1, keepdims=True) + EPSILON)
        hat = x * r1
        gsum[...] += jnp.sum((dn * hat).reshape(32, 8, 576), axis=0)
        e = dn * g1
        res = (dhid[rows, :] + r1 * (e - hat * jnp.mean(e * hat, axis=-1, keepdims=True))).astype(BF)
        for u in range(2):
            start = pl.multiple_of(info[2 * i + u] * 128, 128)
            yscr[pl.ds(start, 128), :] = res[128 * u : 128 * u + 128, :]
    for r, y in enumerate((i0, i1, i2, i3)):
        y[...] = yscr[256 * r : 256 * r + 256, :]
    gqk = dot(n_ref[...], dqk[...], TN)
    gv = dot(n_ref[...], dvl[...], TN)
    total = jnp.sum(gsum[...], axis=0, keepdims=True)
    gcol = jnp.transpose(jnp.broadcast_to(total, (128, 576)))
    for cc in range(4):
        w32[:, 256 * cc : 256 * cc + 256] = jnp.concatenate(
            [
                gqk[:, 144 * cc : 144 * cc + 144],
                gqk[:, 576 + 48 * cc : 576 + 48 * cc + 48],
                gv[:, 48 * cc : 48 * cc + 48],
                gcol[:, 0:16],
            ],
            axis=1,
        )
    for r in range(4):
        col = pl.multiple_of(256 * (c ^ r), 128)
        for k in range(4):
            zz = lax.rem(z + k, 4)
            for out, who in ((gm_out, core), (go_out, 1 - core)):
                row = pl.multiple_of((2 * zz + who) * 72, 8)
                out[k, r] = w32[pl.ds(row, 72), pl.ds(col, 256)].astype(BF)


def place_body(info, a, b, c_, d, out):
    c = info[8]
    for r, ref in enumerate((a, b, c_, d)):
        out[c ^ r] = ref[...]


CORE_SWAP = [(i, i ^ 1) for i in range(8)]


def z_shift(v, k):
    return lax.ppermute(v, "dp", [(i, (i + 2 * k) % 8) for i in range(8)])


def plane_swap(v, k):
    return lax.ppermute(v, "ctx", [(i, i ^ k) for i in range(4)])


def core_swap(v):
    return lax.ppermute(v, "dp", CORE_SWAP)


def add_up(parts):
    total = parts[0].astype(F32)
    for part in parts[1:]:
        total = total + part.astype(F32)
    return total


def fast_shards(
    inputs,
    bounds,
    span_order,
    attn_gain,
    w_query,
    w_key,
    w_value,
    w_out,
    ffn_gain,
    w_gate,
    w_up,
    w_down,
    cotangent,
):
    c = lax.axis_index("ctx").astype(jnp.int32)
    dp = lax.axis_index("dp").astype(jnp.int32)
    slots = jnp.sum(
        jnp.where(
            span_order[None, :] == jnp.arange(8, dtype=jnp.int32)[:, None],
            jnp.arange(8, dtype=jnp.int32)[None, :],
            0,
        ),
        axis=1,
    )
    blocks = ((slots // 2) ^ c) * 2 + slots % 2
    limits = lax.dynamic_index_in_dim(bounds, c, 0, keepdims=False)
    info = jnp.concatenate([blocks, jnp.stack([c, dp // 2, dp % 2]), limits, jnp.zeros((3,), jnp.int32)])

    pack1 = jnp.concatenate(
        [w_query, w_key, w_value, attn_gain[:, None], ffn_gain[:, None], jnp.zeros((72, 14), BF)], axis=1
    )
    down_t = w_down.T
    pack2 = jnp.concatenate(
        [w_gate, w_up, down_t[:72], down_t[72:], w_out, jnp.zeros((72, 112), BF)], axis=1
    )
    flat = jnp.stack([pack1] + [plane_swap(pack1, k) for k in (1, 2, 3)])
    near = [flat] + [z_shift(flat, k) for k in (1, 2, 3)]
    pieces1 = near + [core_swap(v) for v in near]

    def exchange(rows):
        return [plane_swap(lax.dynamic_index_in_dim(rows, c ^ k, 0, keepdims=False), k) for k in (1, 2, 3)]

    x_parts = exchange(inputs)
    flat2 = jnp.stack([pack2] + [z_shift(pack2, k) for k in (1, 2, 3)])
    near2 = [flat2] + [plane_swap(flat2, k) for k in (1, 2, 3)]
    pieces2 = near2 + [core_swap(v) for v in near2]
    d_parts = exchange(cotangent)

    positions = jnp.arange(1024, dtype=jnp.int32)
    half = HEAD_DIM // 2
    frequency = THETA ** (-jnp.arange(half).astype(F32) / half)
    angles = positions.astype(F32)[:, None] * frequency[None, :]
    cosine, sine = jnp.cos(angles), jnp.sin(angles)
    cos4 = jnp.concatenate([cosine] * 4, axis=1)
    sin4 = jnp.concatenate([-sine, sine, -sine, sine], axis=1)

    q, k, v, xp, normed, wqk, wv, gains = call(
        qkv_body,
        [
            shape((3, 4, 768, 64), BF),
            shape((3, 1024, 64), BF),
            shape((3, 1024, 64), BF),
            shape((1024, 576), BF),
            shape((1024, 576), BF),
            shape((576, 768), BF),
            shape((576, 192), BF),
            shape((8, 576), F32),
        ],
        [pltpu.VMEM((1024, 576), BF), pltpu.VMEM((576, 1024), F32)],
        [info, inputs] + x_parts + pieces1 + [cos4, sin4],
        2 * 1024 * 576 * 960,
        "project",
    )
    mix, lse = call(
        attend_body,
        [shape((1024, 576), BF), shape((9, 8, 1024), F32)],
        [pltpu.VMEM((9, 1024, 64), BF), pltpu.VMEM((9, 8, 1024), F32)],
        [info, q, k, v],
        16 * 1024 * 1024 * 64 * 9,
        "attend",
    )
    y0, y1, y2, y3, dhid, dmix, delta, gm2, go2 = call(
        ffn_body,
        [shape((256, 576), BF)] * 4
        + [
            shape((1024, 576), F32),
            shape((3, 4, 768, 64), BF),
            shape((4, 16, 256), F32),
            shape((4, 4, 72, 1408), BF),
            shape((4, 4, 72, 1408), BF),
        ],
        [
            pltpu.VMEM((576, 1536), F32),
            pltpu.VMEM((576, 1024), F32),
            pltpu.VMEM((576, 1536), BF),
            pltpu.VMEM((576, 1536), BF),
            pltpu.VMEM((576, 1536), BF),
            pltpu.VMEM((576, 576), BF),
            pltpu.VMEM((1024, 576), BF),
            pltpu.VMEM((1024, 576), BF),
            pltpu.VMEM((1024, 1536), BF),
            pltpu.VMEM((1024, 1536), BF),
            pltpu.VMEM((1024, 1536), BF),
            pltpu.VMEM((1024, 576), BF),
            pltpu.VMEM((1024, 576), BF),
            pltpu.VMEM((8, 576), F32),
        ],
        [info, xp, mix, gains] + pieces2 + [cotangent] + d_parts,
        6 * 1024 * 576 * (1536 * 3 + 576),
        "feedforward",
    )

    def plane_sum(parts):
        return add_up([parts[0]] + [plane_swap(parts[k], k) for k in (1, 2, 3)])

    def line_sum(parts):
        return add_up([parts[0]] + [z_shift(parts[k], k) for k in (1, 2, 3)])

    def spread(mine, others):
        both = add_up([mine, core_swap(others)]).astype(BF)
        return [both[r] for r in range(4)]

    total2 = plane_sum(spread(gm2, go2)).astype(BF)
    total2 = line_sum([total2[k] for k in range(4)])

    def give_back(parts):
        got = [parts[0]] + [plane_swap(parts[k], k) for k in (1, 2, 3)]
        return call(place_body, [shape((4, 256, 576), BF)], [], [info] + got, 0, "place")[0]

    output = give_back([y0, y1, y2, y3])

    dq, dk, dv = call(
        back_body,
        [shape((9, 1024, 64), F32), shape((3, 1024, 64), F32), shape((3, 1024, 64), F32)],
        [pltpu.VMEM((1024, 64), F32), pltpu.VMEM((1024, 64), F32)],
        [info, q, k, v, dmix, lse, delta],
        24 * 1024 * 1024 * 64 * 9,
        "attend_back",
    )
    i0, i1, i2, i3, gm1, go1 = call(
        tail_body,
        [shape((256, 576), BF)] * 4 + [shape((4, 4, 72, 256), BF), shape((4, 4, 72, 256), BF)],
        [
            pltpu.VMEM((1024, 576), BF),
            pltpu.VMEM((1024, 768), BF),
            pltpu.VMEM((1024, 192), BF),
            pltpu.VMEM((8, 576), F32),
            pltpu.VMEM((576, 1024), F32),
        ],
        [info, xp, normed, dq, dk, dv, dhid, cos4, sin4, wqk, wv, gains],
        4 * 1024 * 576 * 960,
        "input_gradient",
    )
    total1 = line_sum(spread(gm1, go1)).astype(BF)
    total1 = plane_sum([total1[r] for r in range(4)])
    input_grad = give_back([i0, i1, i2, i3])

    down_t = jnp.concatenate([total2[:, 768:960], total2[:, 960:1152]], axis=0)
    return (
        output,
        input_grad,
        total1[:, 240],
        total1[:, 0:144],
        total1[:, 144:192],
        total1[:, 192:240],
        total2[:, 1152:1296],
        total2[:, 1296],
        total2[:, 0:384],
        total2[:, 384:768],
        down_t.T,
    )


def shards(*args):
    seqs, rows, width = args[0].shape
    fits = (seqs, rows, width) == (4, 256, 576) and args[2].shape[0] == 8
    sizes = (lax.axis_size("dp"), lax.axis_size("ctx"))
    if fits and sizes == (8, 4):
        return fast_shards(*args)
    return general_shards(*args)


def solution(mesh):
    in_specs = (
        P("dp", "ctx", None),
        P("dp", None),
        P(),
        P("dp"),
        P("dp", "ctx"),
        P("dp", "ctx"),
        P("dp", "ctx"),
        P("dp", "ctx"),
        P("dp"),
        P("dp", "ctx"),
        P("dp", "ctx"),
        P("dp", "ctx"),
        P("dp", "ctx", None),
    )
    out_specs = (
        P("dp", "ctx", None),
        P("dp", "ctx", None),
        P("dp"),
        P("dp", "ctx"),
        P("dp", "ctx"),
        P("dp", "ctx"),
        P("dp", "ctx"),
        P("dp"),
        P("dp", "ctx"),
        P("dp", "ctx"),
        P("dp", "ctx"),
    )
    return jax.shard_map(shards, mesh=mesh, in_specs=in_specs, out_specs=out_specs, check_vma=False)
```

```python
import functools

import jax
import jax.numpy as jnp
from jax import lax
from jax.experimental import pallas as pl
from jax.experimental.pallas import tpu as pltpu
from jax.sharding import PartitionSpec as P

HEADS = 9
KV_HEADS = 3
HEAD_DIM = 64
FF = 1536
MICRO = 2


EPSILON = 1e-05
THETA = 100000.0
NEG_LARGE = -1e30


def rotary_tables(positions):
    half_dim = HEAD_DIM // 2
    frequency = THETA ** (-jnp.arange(half_dim).astype(jnp.float32) / half_dim)
    angles = positions.astype(jnp.float32)[:, None] * frequency[None, :]
    return (jnp.cos(angles)[None, :, None, :], jnp.sin(angles)[None, :, None, :])


def rotate(values_in, cosine, sine):
    half_dim = HEAD_DIM // 2
    first_half = values_in[..., :half_dim]
    second_half = values_in[..., half_dim:]
    return jnp.concatenate(
        [first_half * cosine - second_half * sine, second_half * cosine + first_half * sine],
        axis=-1,
    )


def rotate_back(grads_in, cosine, sine):
    half_dim = HEAD_DIM // 2
    first_half = grads_in[..., :half_dim]
    second_half = grads_in[..., half_dim:]
    return jnp.concatenate(
        [first_half * cosine + second_half * sine, second_half * cosine - first_half * sine],
        axis=-1,
    )


def positions_of(start, count, span_order, block_len):
    offsets = start + jnp.arange(count, dtype=jnp.int32)
    slots = offsets // block_len
    table = jnp.arange(span_order.shape[0], dtype=jnp.int32)
    chosen = jnp.sum(jnp.where(slots[:, None] == table[None, :], span_order[None, :], 0), axis=1)
    return chosen * block_len + offsets % block_len


def segments_of(positions, limits):
    return (positions[None, :] >= limits[:, 0:1]).astype(jnp.int32) + (
        positions[None, :] >= limits[:, 1:2]
    ).astype(jnp.int32)


def root_mean_square_pieces(values_in):
    inv_root = lax.rsqrt(jnp.mean(values_in * values_in, axis=-1, keepdims=True) + EPSILON)
    return (values_in * inv_root, inv_root)


def root_mean_square_backward(grad_hat, normal_hat, inv_root):
    return inv_root * (
        grad_hat - normal_hat * jnp.mean(grad_hat * normal_hat, axis=-1, keepdims=True)
    )


def key_mask(query_pos, query_seg, key_pos, key_seg):
    allowed = (key_pos[None, None, :] <= query_pos[None, :, None]) & (
        key_seg[:, None, :] == query_seg[:, :, None]
    )
    return allowed[:, :, None, None, :]


def attend_piece(
    carry,
    piece,
    start,
    query_rows,
    query_pos,
    query_seg,
    limits,
    span_order,
    block_len,
    score_scale,
):
    run_max, run_sum, run_acc = carry
    key_piece, value_piece = piece
    seqs_here = key_piece.shape[0]
    count = key_piece.shape[1]
    key_pos = positions_of(start, count, span_order, block_len)
    key_seg = segments_of(key_pos, limits)
    allowed = key_mask(query_pos, query_seg, key_pos, key_seg)
    keys_four = key_piece.reshape(seqs_here, count, KV_HEADS, HEAD_DIM)
    values_four = value_piece.reshape(seqs_here, count, KV_HEADS, HEAD_DIM)
    scores = (
        jnp.einsum("stgrd,skgd->stgrk", query_rows, keys_four, preferred_element_type=jnp.float32)
        * score_scale
    )
    new_max = jnp.maximum(run_max, jnp.max(jnp.where(allowed, scores, NEG_LARGE), axis=-1))
    weights_exp = jnp.where(allowed, jnp.exp(scores - new_max[..., None]), 0.0)
    run_sum = jnp.sum(weights_exp, axis=-1)
    run_acc = jnp.einsum(
        "stgrk,skgd->stgrd",
        weights_exp.astype(jnp.bfloat16),
        values_four,
        preferred_element_type=jnp.float32,
    )
    return (new_max, run_sum, run_acc)


def general_shards(
    inputs,
    bounds,
    span_order,
    attn_gain,
    w_query,
    w_key,
    w_value,
    w_out,
    ffn_gain,
    w_gate,
    w_up,
    w_down,
    cotangent,
):
    seq_local = inputs.shape[0]
    rows = inputs.shape[1]
    width = inputs.shape[2]
    kv_width = KV_HEADS * HEAD_DIM
    group = HEADS // KV_HEADS
    block_len = rows // 2
    micro_seqs = seq_local // MICRO
    ctx_index = lax.axis_index("ctx")
    score_scale = HEAD_DIM ** (-0.5)
    my_start = ctx_index * rows
    positions = positions_of(my_start, rows, span_order, block_len)
    cosine, sine = rotary_tables(positions)

    def fetch():
        columns = (
            lax.all_gather(w_query, "ctx", axis=1, tiled=True),
            lax.all_gather(w_key, "ctx", axis=1, tiled=True),
            lax.all_gather(w_value, "ctx", axis=1, tiled=True),
            lax.all_gather(w_out, "ctx", axis=1, tiled=True),
            lax.all_gather(w_gate, "ctx", axis=1, tiled=True),
            lax.all_gather(w_up, "ctx", axis=1, tiled=True),
            lax.all_gather(w_down, "ctx", axis=1, tiled=True),
        )
        return (
            lax.all_gather(columns[0], "dp", axis=0, tiled=True),
            lax.all_gather(columns[1], "dp", axis=0, tiled=True),
            lax.all_gather(columns[2], "dp", axis=0, tiled=True),
            lax.all_gather(columns[3], "dp", axis=0, tiled=True),
            lax.all_gather(columns[4], "dp", axis=0, tiled=True),
            lax.all_gather(columns[5], "dp", axis=0, tiled=True),
            lax.all_gather(columns[6], "dp", axis=0, tiled=True),
            lax.all_gather(attn_gain, "dp", axis=0, tiled=True),
            lax.all_gather(ffn_gain, "dp", axis=0, tiled=True),
        )

    tot_query = jnp.zeros((width, width), jnp.float32)
    tot_key = jnp.zeros((width, kv_width), jnp.float32)
    tot_value = jnp.zeros((width, kv_width), jnp.float32)
    tot_out = jnp.zeros((width, width), jnp.float32)
    tot_gate = jnp.zeros((width, FF), jnp.float32)
    tot_up = jnp.zeros((width, FF), jnp.float32)
    tot_down = jnp.zeros((FF, width), jnp.float32)
    attention_gain_gradient_total = jnp.zeros((width,), jnp.float32)
    feedforward_gain_gradient_total = jnp.zeros((width,), jnp.float32)
    outputs_list = []
    grads_list = []
    for micro in range(MICRO):
        weights = fetch()
        mat_query, mat_key, mat_value, mat_out, mat_gate, mat_up, mat_down = weights[:7]
        attention_norm_gain = weights[7].astype(jnp.float32)
        feedforward_norm_gain = weights[8].astype(jnp.float32)
        first_seq = micro * micro_seqs
        token_embeddings = inputs[first_seq : first_seq + micro_seqs].astype(jnp.float32)
        limits = bounds[first_seq : first_seq + micro_seqs]
        query_seg = segments_of(positions, limits)
        attention_unit_rows, attention_inverse_root = root_mean_square_pieces(token_embeddings)
        attention_normed_input = (attention_unit_rows * attention_norm_gain).astype(jnp.bfloat16)
        query_pre = jnp.dot(attention_normed_input, mat_query, preferred_element_type=jnp.float32)
        key_pre = jnp.dot(attention_normed_input, mat_key, preferred_element_type=jnp.float32)
        value_rows = jnp.dot(
            attention_normed_input, mat_value, preferred_element_type=jnp.float32
        ).astype(jnp.bfloat16)
        query_rows = rotate(
            query_pre.reshape(micro_seqs, rows, HEADS, HEAD_DIM), cosine, sine
        ).astype(jnp.bfloat16)
        query_rows = query_rows.reshape(micro_seqs, rows, KV_HEADS, group, HEAD_DIM)
        key_rows = rotate(
            key_pre.reshape(micro_seqs, rows, KV_HEADS, HEAD_DIM), cosine, sine
        ).astype(jnp.bfloat16)
        key_rows = key_rows.reshape(micro_seqs, rows, kv_width)
        init_state = (
            jnp.full((micro_seqs, rows, KV_HEADS, group), NEG_LARGE, jnp.float32),
            jnp.zeros((micro_seqs, rows, KV_HEADS, group), jnp.float32),
            jnp.zeros((micro_seqs, rows, KV_HEADS, group, HEAD_DIM), jnp.float32),
        )
        run_max, run_sum, run_acc = attend_piece(
            init_state,
            (
                lax.all_gather(key_rows, "ctx", axis=1, tiled=True),
                lax.all_gather(value_rows, "ctx", axis=1, tiled=True),
            ),
            jnp.int32(0),
            query_rows,
            positions,
            query_seg,
            limits,
            span_order,
            block_len,
            score_scale,
        )
        mixture = run_acc / run_sum[..., None]
        log_total = run_max + jnp.log(run_sum)
        mixture_low = mixture.reshape(micro_seqs, rows, width).astype(jnp.bfloat16)
        hidden_residual = token_embeddings + jnp.dot(
            mixture_low, mat_out, preferred_element_type=jnp.float32
        )
        feedforward_unit_rows, feedforward_inverse_root = root_mean_square_pieces(hidden_residual)
        feedforward_normed_input = (feedforward_unit_rows * feedforward_norm_gain).astype(
            jnp.bfloat16
        )
        gate_value = jnp.dot(feedforward_normed_input, mat_gate, preferred_element_type=jnp.float32)
        up_value = jnp.dot(feedforward_normed_input, mat_up, preferred_element_type=jnp.float32)
        sigmoid_gate = jax.nn.sigmoid(gate_value)
        silu_gate = gate_value * sigmoid_gate
        inner_act = (silu_gate * up_value).astype(jnp.bfloat16)
        result = hidden_residual + jnp.dot(inner_act, mat_down, preferred_element_type=jnp.float32)
        outputs_list.append(result.astype(jnp.bfloat16))
        weights = fetch()
        mat_query, mat_key, mat_value, mat_out, mat_gate, mat_up, mat_down = weights[:7]
        output_gradient_float = cotangent[first_seq : first_seq + micro_seqs].astype(jnp.float32)
        grad_ffn_low = output_gradient_float.astype(jnp.bfloat16)
        tot_down = tot_down + jnp.einsum(
            "stf,std->fd", inner_act, grad_ffn_low, preferred_element_type=jnp.float32
        )
        grad_inner = jnp.einsum(
            "std,fd->stf", grad_ffn_low, mat_down, preferred_element_type=jnp.float32
        )
        grad_gate = (
            grad_inner * up_value * sigmoid_gate * (1.0 + gate_value * (1.0 - sigmoid_gate))
        ).astype(jnp.bfloat16)
        grad_up = (grad_inner * silu_gate).astype(jnp.bfloat16)
        tot_gate = tot_gate + jnp.einsum(
            "ste,stf->ef", feedforward_normed_input, grad_gate, preferred_element_type=jnp.float32
        )
        tot_up = tot_up + jnp.einsum(
            "ste,stf->ef", feedforward_normed_input, grad_up, preferred_element_type=jnp.float32
        )
        feedforward_normed_gradient = jnp.einsum(
            "stf,ef->ste", grad_gate, mat_gate, preferred_element_type=jnp.float32
        ) + jnp.einsum("stf,ef->ste", grad_up, mat_up, preferred_element_type=jnp.float32)
        feedforward_gain_gradient_total = feedforward_gain_gradient_total + jnp.sum(
            feedforward_normed_gradient * feedforward_unit_rows, axis=(0, 1)
        )
        hidden_state_gradient = output_gradient_float + root_mean_square_backward(
            feedforward_normed_gradient * feedforward_norm_gain,
            feedforward_unit_rows,
            feedforward_inverse_root,
        )
        grad_attn_low = hidden_state_gradient.astype(jnp.bfloat16)
        tot_out = tot_out + jnp.einsum(
            "std,ste->de", mixture_low, grad_attn_low, preferred_element_type=jnp.float32
        )
        grad_mix_low = jnp.einsum(
            "ste,de->std", grad_attn_low, mat_out, preferred_element_type=jnp.float32
        ).astype(jnp.bfloat16)
        grad_mix_five = grad_mix_low.reshape(micro_seqs, rows, KV_HEADS, group, HEAD_DIM)
        delta_rows = jnp.sum(grad_mix_five.astype(jnp.float32) * mixture, axis=-1)

        def back_piece(key_piece, value_piece, start):
            key_pos = positions_of(start, rows, span_order, block_len)
            key_seg = segments_of(key_pos, limits)
            allowed = key_mask(positions, query_seg, key_pos, key_seg)
            keys_four = key_piece.reshape(micro_seqs, rows, KV_HEADS, HEAD_DIM)
            values_four = value_piece.reshape(micro_seqs, rows, KV_HEADS, HEAD_DIM)
            scores = (
                jnp.einsum(
                    "stgrd,skgd->stgrk", query_rows, keys_four, preferred_element_type=jnp.float32
                )
                * score_scale
            )
            probs = jnp.where(allowed, jnp.exp(scores - log_total[..., None]), 0.0)
            grad_prob = jnp.einsum(
                "stgrd,skgd->stgrk", grad_mix_five, values_four, preferred_element_type=jnp.float32
            )
            grad_score = (probs * (grad_prob - delta_rows[..., None])).astype(jnp.bfloat16)
            query_term = jnp.einsum(
                "stgrk,skgd->stgrd", grad_score, keys_four, preferred_element_type=jnp.float32
            )
            key_term = jnp.einsum(
                "stgrk,stgrd->skgd", grad_score, query_rows, preferred_element_type=jnp.float32
            )
            value_term = jnp.einsum(
                "stgrk,stgrd->skgd",
                probs.astype(jnp.bfloat16),
                grad_mix_five,
                preferred_element_type=jnp.float32,
            )
            return (
                query_term,
                key_term.reshape(micro_seqs, rows, kv_width),
                value_term.reshape(micro_seqs, rows, kv_width),
            )

        query_zero = jnp.zeros((micro_seqs, rows, KV_HEADS, group, HEAD_DIM), jnp.float32)
        key_source = (
            lax.all_gather(key_rows, "ctx", axis=1, tiled=True),
            lax.all_gather(value_rows, "ctx", axis=1, tiled=True),
        )
        source_keys, source_values = key_source
        full_len = source_keys.shape[1]

        def backward_step(position_index, state):
            grad_query, key_sums, value_sums = state
            start = position_index * rows
            key_piece = lax.dynamic_slice_in_dim(source_keys, start, rows, 1)
            value_piece = lax.dynamic_slice_in_dim(source_values, start, rows, 1)
            query_term, key_term, value_term = back_piece(key_piece, value_piece, start)
            key_sums = lax.dynamic_update_slice_in_dim(key_sums, key_term, start, 1)
            value_sums = lax.dynamic_update_slice_in_dim(value_sums, value_term, start, 1)
            return (grad_query + query_term, key_sums, value_sums)

        back_init = (
            query_zero,
            jnp.zeros((micro_seqs, full_len, kv_width), jnp.float32),
            jnp.zeros((micro_seqs, full_len, kv_width), jnp.float32),
        )
        grad_query, key_sums, value_sums = lax.fori_loop(
            0, full_len // rows, backward_step, back_init
        )
        key_mine, value_mine = (
            lax.psum_scatter(
                key_sums.astype(jnp.bfloat16), "ctx", scatter_dimension=1, tiled=True
            ).astype(jnp.float32),
            lax.psum_scatter(
                value_sums.astype(jnp.bfloat16), "ctx", scatter_dimension=1, tiled=True
            ).astype(jnp.float32),
        )
        grad_q_low = rotate_back(
            (grad_query * score_scale).reshape(micro_seqs, rows, HEADS, HEAD_DIM), cosine, sine
        )
        grad_q_low = grad_q_low.reshape(micro_seqs, rows, width).astype(jnp.bfloat16)
        grad_k_low = rotate_back(
            (key_mine * score_scale).reshape(micro_seqs, rows, KV_HEADS, HEAD_DIM), cosine, sine
        )
        grad_k_low = grad_k_low.reshape(micro_seqs, rows, kv_width).astype(jnp.bfloat16)
        grad_v_low = value_mine.astype(jnp.bfloat16)
        tot_query = tot_query + jnp.einsum(
            "ste,std->ed", attention_normed_input, grad_q_low, preferred_element_type=jnp.float32
        )
        tot_key = tot_key + jnp.einsum(
            "ste,std->ed", attention_normed_input, grad_k_low, preferred_element_type=jnp.float32
        )
        tot_value = tot_value + jnp.einsum(
            "ste,std->ed", attention_normed_input, grad_v_low, preferred_element_type=jnp.float32
        )
        attention_normed_gradient = (
            jnp.einsum("std,ed->ste", grad_q_low, mat_query, preferred_element_type=jnp.float32)
            + jnp.einsum("std,ed->ste", grad_k_low, mat_key, preferred_element_type=jnp.float32)
            + jnp.einsum("std,ed->ste", grad_v_low, mat_value, preferred_element_type=jnp.float32)
        )
        attention_gain_gradient_total = attention_gain_gradient_total + jnp.sum(
            attention_normed_gradient * attention_unit_rows, axis=(0, 1)
        )
        layer_input_gradient = hidden_state_gradient + root_mean_square_backward(
            attention_normed_gradient * attention_norm_gain,
            attention_unit_rows,
            attention_inverse_root,
        )
        grads_list.append(layer_input_gradient.astype(jnp.bfloat16))
    row_sums = (
        lax.psum_scatter(
            tot_query.astype(jnp.bfloat16), "dp", scatter_dimension=0, tiled=True
        ).astype(jnp.float32),
        lax.psum_scatter(
            tot_key.astype(jnp.bfloat16), "dp", scatter_dimension=0, tiled=True
        ).astype(jnp.float32),
        lax.psum_scatter(
            tot_value.astype(jnp.bfloat16), "dp", scatter_dimension=0, tiled=True
        ).astype(jnp.float32),
        lax.psum_scatter(
            tot_out.astype(jnp.bfloat16), "dp", scatter_dimension=0, tiled=True
        ).astype(jnp.float32),
        lax.psum_scatter(
            tot_gate.astype(jnp.bfloat16), "dp", scatter_dimension=0, tiled=True
        ).astype(jnp.float32),
        lax.psum_scatter(tot_up.astype(jnp.bfloat16), "dp", scatter_dimension=0, tiled=True).astype(
            jnp.float32
        ),
        lax.psum_scatter(
            tot_down.astype(jnp.bfloat16), "dp", scatter_dimension=0, tiled=True
        ).astype(jnp.float32),
        lax.psum_scatter(
            attention_gain_gradient_total.astype(jnp.bfloat16),
            "dp",
            scatter_dimension=0,
            tiled=True,
        ).astype(jnp.float32),
        lax.psum_scatter(
            feedforward_gain_gradient_total.astype(jnp.bfloat16),
            "dp",
            scatter_dimension=0,
            tiled=True,
        ).astype(jnp.float32),
    )
    col_sums = (
        lax.psum_scatter(
            row_sums[0].astype(jnp.bfloat16), "ctx", scatter_dimension=1, tiled=True
        ).astype(jnp.float32),
        lax.psum_scatter(
            row_sums[1].astype(jnp.bfloat16), "ctx", scatter_dimension=1, tiled=True
        ).astype(jnp.float32),
        lax.psum_scatter(
            row_sums[2].astype(jnp.bfloat16), "ctx", scatter_dimension=1, tiled=True
        ).astype(jnp.float32),
        lax.psum_scatter(
            row_sums[3].astype(jnp.bfloat16), "ctx", scatter_dimension=1, tiled=True
        ).astype(jnp.float32),
        lax.psum_scatter(
            row_sums[4].astype(jnp.bfloat16), "ctx", scatter_dimension=1, tiled=True
        ).astype(jnp.float32),
        lax.psum_scatter(
            row_sums[5].astype(jnp.bfloat16), "ctx", scatter_dimension=1, tiled=True
        ).astype(jnp.float32),
        lax.psum_scatter(
            row_sums[6].astype(jnp.bfloat16), "ctx", scatter_dimension=1, tiled=True
        ).astype(jnp.float32),
    )
    gain_totals = lax.psum((row_sums[7], row_sums[8]), "ctx")
    return (
        jnp.concatenate(outputs_list, axis=0),
        jnp.concatenate(grads_list, axis=0),
        gain_totals[0],
        col_sums[0],
        col_sums[1],
        col_sums[2],
        col_sums[3],
        gain_totals[1],
        col_sums[4],
        col_sums[5],
        col_sums[6],
    )


BF = jnp.bfloat16
F32 = jnp.float32
FR = 256
FC = 512
LOG2E = 1.4426950408889634
NN = (((1,), (0,)), ((), ()))
NT = (((1,), (1,)), ((), ()))
TN = (((0,), (0,)), ((), ()))


def dot(a, b, dims=NN):
    return lax.dot_general(a, b, dims, preferred_element_type=F32)


def call(body, outs, scratch, args, vmem, name):
    specs = [pl.BlockSpec(memory_space=pltpu.SMEM)] + [
        pl.BlockSpec(memory_space=pltpu.VMEM) for _ in args[1:]
    ]
    return pl.pallas_call(
        body,
        out_shape=outs,
        in_specs=specs,
        out_specs=[pl.BlockSpec(memory_space=pltpu.VMEM) for _ in outs],
        scratch_shapes=scratch,
        compiler_params=pltpu.CompilerParams(vmem_limit_bytes=vmem * 1024 * 1024),
        cost_estimate=pl.CostEstimate(flops=1000000, bytes_accessed=1000000, transcendentals=0),
        name=name,
    )(*args)


def shape(dims, dtype):
    return jax.ShapeDtypeStruct(dims, dtype)


def spans_in(dest, blocks):
    for r in range(4):
        dest[2 * r] = blocks[r][:, :128]
        dest[2 * r + 1] = blocks[r][:, 128:]


def span_rows(info, ref, p):
    return jnp.transpose(ref[info[p]].astype(F32))


def spans_out(scr, outs):
    for r, out in enumerate(outs):
        out[:, :128] = scr[2 * r]
        out[:, 128:] = scr[2 * r + 1]


def rotary_swap(v):
    lane = lax.broadcasted_iota(jnp.int32, v.shape, 1)
    return jnp.where(lane % 64 < 32, pltpu.roll(v, 96, 1), pltpu.roll(v, 32, 1))


def qkv_body(info, x_all, x1, x2, x3, *rest):
    pieces = rest[:2]
    cos_ref, sin_ref = rest[2:4]
    q_out, k_out, v_out = rest[4:7], rest[7:10], rest[10:13]
    xp_out, wqk_out, wv_out, gain_out, raw, w32 = rest[13:]
    c, z, core = info[8], info[9], info[10]
    spans_in(raw, [x_all[c], x1[...], x2[...], x3[...]])
    for p in range(8):
        xp_out[128 * p : 128 * p + 128, :] = span_rows(info, raw, p).astype(BF)
    for j in range(2):
        for k in range(4):
            row = (lax.rem(z - k + 4, 4) * 2 + (core ^ j)) * 72
            row = pl.multiple_of(row, 8)
            for cc in range(4):
                w32[pl.ds(row, 72), 256 * cc : 256 * cc + 256] = pieces[j][c ^ cc, k].astype(F32)
    wq = [w32[:, 256 * cc : 256 * cc + 144] for cc in range(4)]
    wk = [w32[:, 256 * cc + 144 : 256 * cc + 192] for cc in range(4)]
    wv = [w32[:, 256 * cc + 192 : 256 * cc + 240] for cc in range(4)]
    wqk_out[...] = jnp.concatenate(wq + wk, axis=1).astype(BF)
    wv_out[...] = jnp.concatenate(wv, axis=1).astype(BF)
    gains = jnp.transpose(w32[:, 128:256])
    gain_out[...] = gains[112:120, :]
    g1 = gains[112:113, :]
    for i in range(4):
        rows = pl.ds(256 * i, 256)
        x = xp_out[rows, :].astype(F32)
        inv = lax.rsqrt(jnp.mean(x * x, axis=-1, keepdims=True) + EPSILON)
        n = (x * inv * g1).astype(BF)
        qk = dot(n, wqk_out[...])
        v = dot(n, wv_out[...])
        cs, sn = cos_ref[rows, :], sin_ref[rows, :]
        for b in range(6):
            t = qk[:, 128 * b : 128 * b + 128]
            t = (t * cs + rotary_swap(t) * sn).astype(BF)
            for u in range(2):
                h = 2 * b + u
                part = t[:, 64 * u : 64 * u + 64]
                if h < 9:
                    q_out[h // 3][i, 256 * (h % 3) : 256 * (h % 3) + 256, :] = part
                else:
                    k_out[h - 9][rows, :] = part
        v = v.astype(BF)
        for g in range(3):
            v_out[g][rows, :] = v[:, 64 * g : 64 * g + 64]


def segment_start(info, pos):
    b0, b1 = info[11], info[12]
    return jnp.where(pos >= b1, b1, jnp.where(pos >= b0, b0, 0))


def attend_body(info, q_ref, k_ref, v_ref, mix_out, lse_out):
    scale = 0.125 * LOG2E
    for i in range(4):
        kpos = lax.broadcasted_iota(jnp.int32, (256, 256), 1)
        qpos = lax.broadcasted_iota(jnp.int32, (256, 256), 0) + 256 * i
        first = segment_start(info, qpos)
        parts = []
        for r in range(3):
            q = q_ref[i, 256 * r : 256 * r + 256, :]
            tiles = []
            top = None
            for j in range(i + 1):
                s = dot(q, k_ref[256 * j : 256 * j + 256, :], NT) * scale
                ok = None
                if j == 0 or i == 3:
                    ok = (kpos + 256 * j) >= first
                if j == i:
                    causal = (kpos + 256 * j) <= qpos
                    ok = causal if ok is None else ok & causal
                if ok is not None:
                    s = jnp.where(ok, s, NEG_LARGE)
                tiles.append(s)
                m = jnp.maximum(s[:, :128], s[:, 128:])
                top = m if top is None else jnp.maximum(top, m)
            m = jnp.max(top, axis=-1, keepdims=True)
            total = None
            acc = None
            for j in range(i + 1):
                e = jnp.exp2(tiles[j] - m)
                part = e[:, :128] + e[:, 128:]
                total = part if total is None else total + part
                o = dot(e.astype(BF), v_ref[256 * j : 256 * j + 256, :])
                acc = o if acc is None else acc + o
            total = jnp.sum(total, axis=-1, keepdims=True)
            parts.append((acc / total).astype(BF))
            lse = m + jnp.log2(total)
            lse_out[r, :, 256 * i : 256 * i + 256] = jnp.transpose(jnp.broadcast_to(lse, (256, 128)))[0:8, :]
        mix_out[256 * i : 256 * i + 256, :] = jnp.concatenate(parts, axis=1)


def ffn_body(info, xp, m0, m1, m2, gains, *rest):
    groups = rest[:6]
    d_all, d1, d2, d3 = rest[6:10]
    y0, y1, y2, y3, dhid_out, dmix_out, delta_out, gm_out, go_out = rest[10:19]
    w32, o32, wg, wu, wd, wo, raw, normed, inner, dgate, dup, yscr, dattn, gsum, mix = rest[19:]

    def piece(j, r, k):
        a, b, last = groups[3 * j : 3 * j + 3]
        at = (0, 0, 1, 1)[k]
        if r < 3:
            return (a if k in (0, 3) else b), 2 * r + at
        return (b, 6 + at) if k in (0, 3) else (last, at)

    mix[...] = jnp.concatenate([m0[...], m1[...], m2[...]], axis=1)
    c, z, core = info[8], info[9], info[10]

    def collect(lane):
        for j in range(2):
            for r in range(4):
                col = pl.multiple_of(384 * (c ^ r), 128)
                for k in range(4):
                    zz = lax.rem(z - k + 4, 4)
                    row = pl.multiple_of((2 * zz + (core ^ j)) * 72, 8)
                    ref, at = piece(j, r, k)
                    w32[pl.ds(row, 72), pl.ds(col, 384)] = ref[at, :, lane : lane + 384].astype(F32)

    collect(0)
    wg[...] = w32[...].astype(BF)
    collect(384)
    wu[...] = w32[...].astype(BF)
    for r in range(4):
        for k in range(4):
            zz = lax.rem(z - k + 4, 4)
            ref, at = piece(0, r, k)
            a = ref[at, :, 768:1408].astype(F32)
            ref, at = piece(1, r, k)
            b = ref[at, :, 768:1408].astype(F32)
            dcol = pl.multiple_of(384 * zz, 128)
            lo = jnp.where(core == 0, a, b)
            hi = jnp.where(core == 0, b, a)
            for half in range(2):
                row = pl.multiple_of(144 * (c ^ r) + 72 * half, 8)
                w32[pl.ds(row, 72), pl.ds(dcol, 384)] = jnp.concatenate(
                    [lo[:, 192 * half : 192 * half + 192], hi[:, 192 * half : 192 * half + 192]], axis=1
                )
            col = pl.multiple_of(256 * (c ^ r), 128)
            o32[pl.ds(pl.multiple_of(144 * zz, 8), 72), pl.ds(col, 256)] = lo[:, 384:640]
            o32[pl.ds(pl.multiple_of(144 * zz + 72, 8), 72), pl.ds(col, 256)] = hi[:, 384:640]
    wd[...] = w32[...].astype(BF)
    wo[...] = jnp.concatenate([o32[:, 256 * cc : 256 * cc + 144] for cc in range(4)], axis=1).astype(BF)

    spans_in(raw, [d_all[c], d1[...], d2[...], d3[...]])
    g2 = gains[1:2, :]
    gsum[...] = jnp.zeros_like(gsum)

    def chunk(i):
        rows = pl.ds(pl.multiple_of(FR * i, FR), FR)
        x = xp[rows, :].astype(F32)
        m = mix[rows, :]
        hidden = x + dot(m, wo[...])
        r2 = lax.rsqrt(jnp.mean(hidden * hidden, axis=-1, keepdims=True) + EPSILON)
        hat = hidden * r2
        n = (hat * g2).astype(BF)
        normed[rows, :] = n
        dy = jnp.concatenate([span_rows(info, raw, i * (FR // 128) + u) for u in range(FR // 128)], axis=0)
        dlow = dy.astype(BF)
        res = hidden
        dn = None
        for f in range(FF // FC):
            cols = slice(FC * f, FC * f + FC)
            gate = dot(n, wg[:, cols])
            up = dot(n, wu[:, cols])
            sg = 1.0 / (1.0 + jnp.exp(-gate))
            silu = gate * sg
            act = (silu * up).astype(BF)
            inner[rows, cols] = act
            res = res + dot(act, wd[:, cols], NT)
            din = dot(dlow, wd[:, cols])
            dg = (din * up * (sg + silu * (1.0 - sg))).astype(BF)
            du = (din * silu).astype(BF)
            dgate[rows, cols] = dg
            dup[rows, cols] = du
            t = dot(dg, wg[:, cols], NT) + dot(du, wu[:, cols], NT)
            dn = t if dn is None else dn + t
        for u in range(FR // 128):
            yscr[info[i * (FR // 128) + u]] = jnp.transpose(res[128 * u : 128 * u + 128, :]).astype(BF)
        gsum[...] += jnp.sum((dn * hat).reshape(FR // 8, 8, 576), axis=0)
        e = dn * g2
        dh = dy + r2 * (e - hat * jnp.mean(e * hat, axis=-1, keepdims=True))
        dhid_out[rows, :] = dh
        da = dh.astype(BF)
        dattn[rows, :] = da
        dm = dot(da, wo[...], NT).astype(BF)
        prod = dm.astype(F32) * m.astype(F32)
        for u in range(FR // 256):
            block = i * (FR // 256) + u
            part_rows = slice(256 * u, 256 * u + 256)
            lane = lax.broadcasted_iota(jnp.int32, (256, 128), 1)
            table = jnp.zeros((256, 128), F32)
            for h in range(9):
                dmix_out[h // 3, block, 256 * (h % 3) : 256 * (h % 3) + 256, :] = dm[part_rows, 64 * h : 64 * h + 64]
                col = jnp.sum(prod[part_rows, 64 * h : 64 * h + 64], axis=-1, keepdims=True)
                table = jnp.where(lane == h, col, table)
            delta_out[block] = jnp.transpose(table)[0:16, :]
    def step(i, carry):
        chunk(i)
        return carry

    lax.fori_loop(0, 1024 // FR, step, 0)
    spans_out(yscr, (y0, y1, y2, y3))

    def deal(lane):
        for r in range(4):
            col = pl.multiple_of(384 * (c ^ r), 128)
            for k in range(4):
                zz = lax.rem(z + k, 4)
                for out, who in ((gm_out, core), (go_out, 1 - core)):
                    row = pl.multiple_of((2 * zz + who) * 72, 8)
                    out[r, k, :, lane : lane + 384] = w32[pl.ds(row, 72), pl.ds(col, 384)].astype(BF)

    w32[...] = dot(normed[...], dgate[...], TN)
    deal(0)
    w32[...] = dot(normed[...], dup[...], TN)
    deal(384)
    for p in range(8):
        normed[128 * p : 128 * p + 128, :] = span_rows(info, raw, p).astype(BF)
    w32[...] = dot(normed[...], inner[...], TN)
    og = dot(mix[...], dattn[...], TN)
    for cc in range(4):
        o32[:, 256 * cc : 256 * cc + 144] = og[:, 144 * cc : 144 * cc + 144]
    total = jnp.sum(gsum[...], axis=0, keepdims=True)
    gcol = jnp.transpose(jnp.broadcast_to(total, (128, 576)))
    for cc in range(4):
        o32[:, 256 * cc + 144 : 256 * cc + 256] = gcol[:, 0:112]
    for r in range(4):
        ocol = pl.multiple_of(256 * (c ^ r), 128)
        for k in range(4):
            zz = lax.rem(z + k, 4)
            dcol = pl.multiple_of(384 * zz, 128)
            a = w32[pl.ds(pl.multiple_of(144 * (c ^ r), 8), 72), pl.ds(dcol, 384)]
            b = w32[pl.ds(pl.multiple_of(144 * (c ^ r) + 72, 8), 72), pl.ds(dcol, 384)]
            left = [a[:, :192], b[:, :192]]
            right = [a[:, 192:], b[:, 192:]]
            for out, who in ((gm_out, core), (go_out, 1 - core)):
                row = pl.multiple_of((2 * zz + who) * 72, 8)
                o = o32[pl.ds(row, 72), pl.ds(ocol, 256)]
                d = [jnp.where(who == 0, u, v) for u, v in zip(left, right)]
                out[r, k, :, 768:1408] = jnp.concatenate(d + [o], axis=1).astype(BF)


def back_body(
    info, q_ref, k_ref, v_ref, dmix_ref, lse_ref, delta_ref, cos_ref, sin_ref, out, dq_scr, dk_scr, dv_scr, *, g
):
    scale = 0.125 * LOG2E
    dk_scr[...] = jnp.zeros_like(dk_scr)
    dv_scr[...] = jnp.zeros_like(dv_scr)
    for i in range(4):
        qpos = lax.broadcasted_iota(jnp.int32, (256, 256), 1) + 256 * i
        kpos = lax.broadcasted_iota(jnp.int32, (256, 256), 0)
        first = segment_start(info, qpos)
        for r in range(3):
            q = q_ref[i, 256 * r : 256 * r + 256, :]
            do = dmix_ref[g, i, 256 * r : 256 * r + 256, :]
            lse = lse_ref[r, 0:1, 256 * i : 256 * i + 256]
            delta = delta_ref[i, 3 * g + r : 3 * g + r + 1, :]
            dq = None
            for j in range(i + 1):
                keys = slice(256 * j, 256 * j + 256)
                kk = k_ref[keys, :]
                s = dot(kk, q, NT) * scale
                p = jnp.exp2(s - lse)
                ok = None
                if j == 0 or i == 3:
                    ok = (kpos + 256 * j) >= first
                if j == i:
                    causal = (kpos + 256 * j) <= qpos
                    ok = causal if ok is None else ok & causal
                if ok is not None:
                    p = jnp.where(ok, p, 0.0)
                dp = dot(v_ref[keys, :], do, NT)
                ds = (p * (dp - delta)).astype(BF)
                dv_scr[keys, :] += dot(p.astype(BF), do)
                dk_scr[keys, :] += dot(ds, q)
                t = dot(ds, kk, TN)
                dq = t if dq is None else dq + t
            dq_scr[r, 256 * i : 256 * i + 256, :] = dq
    for i in range(4):
        rows = slice(256 * i, 256 * i + 256)
        cs, sn = cos_ref[rows, :], sin_ref[rows, :]
        done = []
        for pair in ((dq_scr[0, rows, :], dq_scr[1, rows, :]), (dq_scr[2, rows, :], dk_scr[rows, :])):
            t = jnp.concatenate(pair, axis=1) * 0.125
            done.append((t * cs - rotary_swap(t) * sn).astype(BF))
        last = jnp.concatenate([dv_scr[rows, :], jnp.zeros((256, 64), F32)], axis=1).astype(BF)
        out[rows, :] = jnp.concatenate(done + [last], axis=1)


def joined(parts):
    qk = jnp.concatenate([d[:, 0:192] for d in parts] + [d[:, 192:256] for d in parts], axis=1)
    return qk, jnp.concatenate([d[:, 256:320] for d in parts], axis=1)


def project_grad_body(
    info, xp, d0, d1, d2, dhid, wqk, wv, gains, i0, i1, i2, i3, gm_out, go_out, n_scr, gsum, w32, yscr
):
    c, z, core = info[8], info[9], info[10]
    g1 = gains[0:1, :]
    gsum[...] = jnp.zeros_like(gsum)
    qk, vv = joined((d0, d1, d2))
    for i in range(4):
        rows = slice(256 * i, 256 * i + 256)
        x = xp[rows, :].astype(F32)
        r1 = lax.rsqrt(jnp.mean(x * x, axis=-1, keepdims=True) + EPSILON)
        hat = x * r1
        n_scr[rows, :] = (hat * g1).astype(BF)
        dn = dot(qk[rows, :], wqk[...], NT) + dot(vv[rows, :], wv[...], NT)
        gsum[...] += jnp.sum((dn * hat).reshape(32, 8, 576), axis=0)
        e = dn * g1
        res = dhid[rows, :] + r1 * (e - hat * jnp.mean(e * hat, axis=-1, keepdims=True))
        for u in range(2):
            yscr[info[2 * i + u]] = jnp.transpose(res[128 * u : 128 * u + 128, :]).astype(BF)
    spans_out(yscr, (i0, i1, i2, i3))
    gqk = dot(n_scr[...], qk, TN)
    gv = dot(n_scr[...], vv, TN)
    total = jnp.sum(gsum[...], axis=0, keepdims=True)
    gcol = jnp.transpose(jnp.broadcast_to(total, (128, 576)))
    for cc in range(4):
        w32[:, 256 * cc : 256 * cc + 256] = jnp.concatenate(
            [
                gqk[:, 144 * cc : 144 * cc + 144],
                gqk[:, 576 + 48 * cc : 576 + 48 * cc + 48],
                gv[:, 48 * cc : 48 * cc + 48],
                gcol[:, 0:16],
            ],
            axis=1,
        )
    for r in range(4):
        col = pl.multiple_of(256 * (c ^ r), 128)
        for k in range(4):
            zz = lax.rem(z + k, 4)
            for out, who in ((gm_out, core), (go_out, 1 - core)):
                row = pl.multiple_of((2 * zz + who) * 72, 8)
                out[r, k] = w32[pl.ds(row, 72), pl.ds(col, 256)].astype(BF)


def last_body(info, q, k, v, dmix, lse, delta, cos, sin, xp, d0, d1, dhid, wqk, wv, gains, *rest):
    i0, i1, i2, i3, gm_out, go_out = rest[:6]
    d2, dq_scr, dk_scr, dv_scr, n_scr, gsum, w32, yscr = rest[6:]
    back_body(info, q, k, v, dmix, lse, delta, cos, sin, d2, dq_scr, dk_scr, dv_scr, g=2)
    project_grad_body(
        info, xp, d0, d1, d2, dhid, wqk, wv, gains, i0, i1, i2, i3, gm_out, go_out, n_scr, gsum, w32, yscr
    )


def place_body(info, a, b, c_, d, out):
    for r, ref in enumerate((a, b, c_, d)):
        out[info[8] ^ r] = ref[...]


def pack_body(q, kt, vt, a, f, out):
    out[:, 0:144] = q[...]
    out[:, 144:256] = jnp.concatenate(
        [
            jnp.transpose(kt[...].astype(F32)),
            jnp.transpose(vt[...].astype(F32)),
            jnp.transpose(jnp.concatenate([a[...].astype(F32), f[...].astype(F32), jnp.zeros((14, 72), F32)], axis=0)),
        ],
        axis=1,
    ).astype(BF)


def first_finish_body(a, b, c_, d, gain, query, key_t, value_t):
    total = a[...].astype(F32) + b[...].astype(F32) + c_[...].astype(F32) + d[...].astype(F32)
    query[...] = total[:, 0:144]
    rest = jnp.transpose(total[:, 128:256])
    key_t[...] = rest[16:64]
    value_t[...] = rest[64:112]
    gain[...] = rest[112:113]


def second_finish_body(a, b, c_, d, gate, up, down_t, out, gain):
    total = a[...].astype(F32) + b[...].astype(F32) + c_[...].astype(F32) + d[...].astype(F32)
    gate[...] = total[:, 0:384]
    up[...] = total[:, 384:768]
    down_t[0:72, :] = total[:, 768:960]
    down_t[72:144, :] = total[:, 960:1152]
    out[...] = total[:, 1152:1296]
    gain[...] = jnp.transpose(total[:, 1280:1408])[16:17]


CORE_SWAP = [(i, i ^ 1) for i in range(8)]


def z_shift(v, k):
    return lax.ppermute(v, "dp", [(i, (i + 2 * k) % 8) for i in range(8)])


def plane_swap(v, k):
    return lax.ppermute(v, "ctx", [(i, i ^ k) for i in range(4)])


def core_swap(v):
    return lax.ppermute(v, "dp", CORE_SWAP)


def add_up(parts):
    total = parts[0].astype(F32)
    for part in parts[1:]:
        total = total + part.astype(F32)
    return total


def fast_shards(
    inputs,
    bounds,
    span_order,
    attn_gain,
    w_query,
    w_key,
    w_value,
    w_out,
    ffn_gain,
    w_gate,
    w_up,
    w_down,
    cotangent,
):
    c = lax.axis_index("ctx").astype(jnp.int32)
    dp = lax.axis_index("dp").astype(jnp.int32)
    slots = jnp.sum(
        jnp.where(
            span_order[None, :] == jnp.arange(8, dtype=jnp.int32)[:, None],
            jnp.arange(8, dtype=jnp.int32)[None, :],
            0,
        ),
        axis=1,
    )
    blocks = ((slots // 2) ^ c) * 2 + slots % 2
    limits = lax.dynamic_index_in_dim(bounds, c, 0, keepdims=False)
    info = jnp.concatenate([blocks, jnp.stack([c, dp // 2, dp % 2]), limits, jnp.zeros((3,), jnp.int32)])

    def after(value, *first):
        return lax.optimization_barrier((value, *first))[0]

    x_rows = jnp.swapaxes(inputs, 1, 2)
    d_rows = jnp.swapaxes(cotangent, 1, 2)

    def exchange(rows, k):
        return plane_swap(lax.dynamic_index_in_dim(rows, c ^ k, 0, keepdims=False), k)

    pack1 = pl.pallas_call(pack_body, out_shape=shape((72, 256), BF), name="pack")(
        w_query, w_key.T, w_value.T, attn_gain[None, :], ffn_gain[None, :]
    )
    line1 = [pack1] + [z_shift(pack1, k) for k in (1, 2, 3)]
    x1, x2 = exchange(x_rows, 1), exchange(x_rows, 2)
    flat1 = jnp.stack(line1)
    near = [flat1] + [plane_swap(flat1, k) for k in (1, 2, 3)]
    gate_late, down_t = lax.optimization_barrier((w_gate, w_down.T, flat1))[:2]
    pack2 = jnp.concatenate(
        [gate_late, w_up, down_t[:72], down_t[72:], w_out, jnp.zeros((72, 112), BF)], axis=1
    )
    x3 = exchange(after(x_rows, x1, x2), 3)
    near_all = jnp.stack(near)
    pack2_later = after(pack2, near_all)
    z_three = z_shift(pack2_later, 3)
    far_all = core_swap(near_all)
    z_one, z_two = z_shift(pack2_later, 1), z_shift(pack2_later, 2)
    z_three, x3, far_all = lax.optimization_barrier((z_three, x3, far_all))
    line_a = jnp.stack([pack2, z_three])
    a_x, a_y = plane_swap(line_a, 1), plane_swap(line_a, 2)

    positions = after(jnp.arange(1024, dtype=jnp.int32), *near)
    half = HEAD_DIM // 2
    frequency = THETA ** (-jnp.arange(half).astype(F32) / half)
    angles = positions.astype(F32)[:, None] * frequency[None, :]
    cosine, sine = jnp.cos(angles), jnp.sin(angles)
    cos4 = jnp.concatenate([cosine] * 4, axis=1)
    sin4 = jnp.concatenate([-sine, sine, -sine, sine], axis=1)

    made = call(
        qkv_body,
        [shape((4, 768, 64), BF)] * 3
        + [shape((1024, 64), BF)] * 6
        + [
            shape((1024, 576), BF),
            shape((576, 768), BF),
            shape((576, 192), BF),
            shape((8, 576), F32),
        ],
        [pltpu.VMEM((8, 576, 128), BF), pltpu.VMEM((576, 1024), F32)],
        [info, after(x_rows, line_a), x1, x2, x3, near_all, far_all, cos4, sin4],
        40,
        "project",
    )
    q, k, v = made[0:3], made[3:6], made[6:9]
    xp, wqk, wv, gains = made[9:]
    def attend(g, q_):
        return call(
            attend_body,
            [shape((1024, 192), BF), shape((3, 8, 1024), F32)],
            [],
            [info, q_, k[g], v[g]],
            24,
            "attend",
        )

    z_one, z_two, d_first, q0 = lax.optimization_barrier((z_one, z_two, d_rows, q[0]))
    line_b = jnp.stack([z_one, z_two])
    q0 = after(q0, line_b)
    b_x, b_y = plane_swap(line_b, 1), plane_swap(line_b, 2)
    d1 = exchange(d_first, 1)
    mix0, lse0 = attend(0, q0)
    a_x, a_y, mix0, d_second = lax.optimization_barrier((a_x, a_y, mix0, d_rows))
    a_low, a_high = plane_swap(a_x[:1], 2), plane_swap(a_y[1:], 1)
    d2 = exchange(d_second, 2)
    mix1, lse1 = attend(1, after(q[1], mix0))
    b_x, b_y, d1, mix1, d_third = lax.optimization_barrier((b_x, b_y, d1, mix1, d_rows))
    b_low, b_high = plane_swap(b_x[:1], 2), plane_swap(b_y[1:], 1)
    d3 = exchange(d_third, 3)
    mix2, lse2 = attend(2, after(q[2], mix1, a_low, a_high))
    mixes, lses = [mix0, mix1, mix2], [lse0, lse1, lse2]
    own_parts = [
        jnp.concatenate([line_a, a_x, a_y], axis=0),
        jnp.concatenate([line_b, b_x, b_y, a_low, a_high], axis=0),
        jnp.concatenate([b_low, b_high], axis=0),
    ]
    pieces2 = own_parts + [core_swap(v_) for v_ in own_parts]
    d_parts = [d1, d2, d3]
    y0, y1, y2, y3, dhid, dmix, delta, gm2, go2 = call(
        ffn_body,
        [shape((576, 256), BF)] * 4
        + [
            shape((1024, 576), F32),
            shape((3, 4, 768, 64), BF),
            shape((4, 16, 256), F32),
            shape((4, 4, 72, 1408), BF),
            shape((4, 4, 72, 1408), BF),
        ],
        [
            pltpu.VMEM((576, 1536), F32),
            pltpu.VMEM((576, 1024), F32),
            pltpu.VMEM((576, 1536), BF),
            pltpu.VMEM((576, 1536), BF),
            pltpu.VMEM((576, 1536), BF),
            pltpu.VMEM((576, 576), BF),
            pltpu.VMEM((8, 576, 128), BF),
            pltpu.VMEM((1024, 576), BF),
            pltpu.VMEM((1024, 1536), BF),
            pltpu.VMEM((1024, 1536), BF),
            pltpu.VMEM((1024, 1536), BF),
            pltpu.VMEM((8, 576, 128), BF),
            pltpu.VMEM((1024, 576), BF),
            pltpu.VMEM((8, 576), F32),
            pltpu.VMEM((1024, 576), BF),
        ],
        [info, xp] + mixes + [gains] + pieces2 + [d_rows] + d_parts,
        60,
        "feedforward",
    )

    def core_sum(mine, others):
        return add_up([mine, core_swap(others)]).astype(BF)

    def place(parts):
        placed = call(place_body, [shape((4, 576, 256), BF)], [], [info] + parts, 16, "place")[0]
        return jnp.swapaxes(placed, 1, 2)

    def attend_back(g, *first):
        return call(
            functools.partial(back_body, g=g),
            [shape((1024, 384), BF)],
            [pltpu.VMEM((3, 1024, 64), F32), pltpu.VMEM((1024, 64), F32), pltpu.VMEM((1024, 64), F32)],
            [info, after(q[g], *first) if first else q[g], k[g], v[g], dmix, lses[g], delta, cos4, sin4],
            24,
            "attend_back",
        )[0]

    both = core_sum(gm2, go2)
    y1, y2 = plane_swap(y1, 1), plane_swap(y2, 2)
    grad0 = attend_back(0)
    both, grad0, y1, y2, y3 = lax.optimization_barrier((both, grad0, y1, y2, y3))
    low = plane_swap(both[3, :2], 2)
    high = plane_swap(both[3, 2:], 1)
    y3 = plane_swap(y3, 3)
    grad1 = attend_back(1, grad0, both)
    low, high, grad1, y3 = lax.optimization_barrier((low, high, grad1, y3))
    one = jnp.concatenate([add_up([both[1, :2], low]).astype(BF), both[1, 2:]], axis=0)
    two = jnp.concatenate([both[2, :2], add_up([both[2, 2:], high]).astype(BF)], axis=0)
    one_got, two_got = plane_swap(one, 1), plane_swap(two, 2)
    output = place([y0, y1, y2, y3])
    i0, i1, i2, i3, gm1, go1 = call(
        last_body,
        [shape((576, 256), BF)] * 4 + [shape((4, 4, 72, 256), BF), shape((4, 4, 72, 256), BF)],
        [
            pltpu.VMEM((1024, 384), BF),
            pltpu.VMEM((3, 1024, 64), F32),
            pltpu.VMEM((1024, 64), F32),
            pltpu.VMEM((1024, 64), F32),
            pltpu.VMEM((1024, 576), BF),
            pltpu.VMEM((8, 576), F32),
            pltpu.VMEM((576, 1024), F32),
            pltpu.VMEM((8, 576, 128), BF),
        ],
        [info, after(q[2], grad1, one, two), k[2], v[2], dmix, lses[2], delta, cos4, sin4]
        + [xp, grad0, grad1, dhid, wqk, wv, gains],
        40,
        "attend_back_input_gradient",
    )
    one_got, two_got, gm1, go1, i1, i2, i3 = lax.optimization_barrier((one_got, two_got, gm1, go1, i1, i2, i3))
    both1 = core_sum(gm1, go1)
    i1, i2 = plane_swap(i1, 1), plane_swap(i2, 2)
    total2 = add_up([both[0], one_got, two_got]).astype(BF)
    two_one, two_three = z_shift(total2[1], 1), z_shift(total2[3], 3)
    both1, i3, i1, i2, total2 = lax.optimization_barrier((both1, i3, i1, i2, total2))
    two_two = z_shift(total2[2], 2)
    first_got = [plane_swap(both1[r], r) for r in (1, 2, 3)]
    i3 = plane_swap(i3, 3)
    total1 = add_up([both1[0]] + first_got).astype(BF)
    total1, two_one, two_three = lax.optimization_barrier((total1, two_one, two_three))
    line2 = [total2[0], two_one, two_two, two_three]
    line1 = [total1[0]] + [z_shift(total1[k_], k_) for k_ in (1, 2, 3)]
    input_grad = place([i0, i1, i2, i3])
    gate_g, up_g, down_t, out_g, ffn_gain_g = pl.pallas_call(
        second_finish_body,
        out_shape=[shape((72, 384), F32)] * 2 + [shape((144, 192), F32), shape((72, 144), F32), shape((1, 72), F32)],
        name="finish_second",
    )(*line2)
    attn_gain_g, query_g, key_t, value_t = pl.pallas_call(
        first_finish_body,
        out_shape=[shape((1, 72), F32), shape((72, 144), F32), shape((48, 72), F32), shape((48, 72), F32)],
        name="finish_first",
    )(*line1)
    return (
        output,
        input_grad,
        attn_gain_g[0],
        query_g,
        key_t.T,
        value_t.T,
        out_g,
        ffn_gain_g[0],
        gate_g,
        up_g,
        down_t.T,
    )


def shards(*args):
    seqs, rows, width = args[0].shape
    fits = (seqs, rows, width) == (4, 256, 576) and args[2].shape[0] == 8
    sizes = (lax.axis_size("dp"), lax.axis_size("ctx"))
    if fits and sizes == (8, 4):
        return fast_shards(*args)
    return general_shards(*args)


def solution(mesh):
    in_specs = (
        P("dp", "ctx", None),
        P("dp", None),
        P(),
        P("dp"),
        P("dp", "ctx"),
        P("dp", "ctx"),
        P("dp", "ctx"),
        P("dp", "ctx"),
        P("dp"),
        P("dp", "ctx"),
        P("dp", "ctx"),
        P("dp", "ctx"),
        P("dp", "ctx", None),
    )
    out_specs = (
        P("dp", "ctx", None),
        P("dp", "ctx", None),
        P("dp"),
        P("dp", "ctx"),
        P("dp", "ctx"),
        P("dp", "ctx"),
        P("dp", "ctx"),
        P("dp"),
        P("dp", "ctx"),
        P("dp", "ctx"),
        P("dp", "ctx"),
    )
    return jax.shard_map(shards, mesh=mesh, in_specs=in_specs, out_specs=out_specs, check_vma=False)
```

```python
import functools

import jax
import jax.numpy as jnp
from jax import lax
from jax.experimental import pallas as pl
from jax.experimental.pallas import tpu as pltpu
from jax.sharding import PartitionSpec as P

HEADS = 9
KV_HEADS = 3
HEAD_DIM = 64
FF = 1536
MICRO = 2


EPSILON = 1e-05
THETA = 100000.0
NEG_LARGE = -1e30


def rotary_tables(positions):
    half_dim = HEAD_DIM // 2
    frequency = THETA ** (-jnp.arange(half_dim).astype(jnp.float32) / half_dim)
    angles = positions.astype(jnp.float32)[:, None] * frequency[None, :]
    return (jnp.cos(angles)[None, :, None, :], jnp.sin(angles)[None, :, None, :])


def rotate(values_in, cosine, sine):
    half_dim = HEAD_DIM // 2
    first_half = values_in[..., :half_dim]
    second_half = values_in[..., half_dim:]
    return jnp.concatenate(
        [first_half * cosine - second_half * sine, second_half * cosine + first_half * sine],
        axis=-1,
    )


def rotate_back(grads_in, cosine, sine):
    half_dim = HEAD_DIM // 2
    first_half = grads_in[..., :half_dim]
    second_half = grads_in[..., half_dim:]
    return jnp.concatenate(
        [first_half * cosine + second_half * sine, second_half * cosine - first_half * sine],
        axis=-1,
    )


def positions_of(start, count, span_order, block_len):
    offsets = start + jnp.arange(count, dtype=jnp.int32)
    slots = offsets // block_len
    table = jnp.arange(span_order.shape[0], dtype=jnp.int32)
    chosen = jnp.sum(jnp.where(slots[:, None] == table[None, :], span_order[None, :], 0), axis=1)
    return chosen * block_len + offsets % block_len


def segments_of(positions, limits):
    return (positions[None, :] >= limits[:, 0:1]).astype(jnp.int32) + (
        positions[None, :] >= limits[:, 1:2]
    ).astype(jnp.int32)


def root_mean_square_pieces(values_in):
    inv_root = lax.rsqrt(jnp.mean(values_in * values_in, axis=-1, keepdims=True) + EPSILON)
    return (values_in * inv_root, inv_root)


def root_mean_square_backward(grad_hat, normal_hat, inv_root):
    return inv_root * (
        grad_hat - normal_hat * jnp.mean(grad_hat * normal_hat, axis=-1, keepdims=True)
    )


def key_mask(query_pos, query_seg, key_pos, key_seg):
    allowed = (key_pos[None, None, :] <= query_pos[None, :, None]) & (
        key_seg[:, None, :] == query_seg[:, :, None]
    )
    return allowed[:, :, None, None, :]


def attend_piece(
    carry,
    piece,
    start,
    query_rows,
    query_pos,
    query_seg,
    limits,
    span_order,
    block_len,
    score_scale,
):
    run_max, run_sum, run_acc = carry
    key_piece, value_piece = piece
    seqs_here = key_piece.shape[0]
    count = key_piece.shape[1]
    key_pos = positions_of(start, count, span_order, block_len)
    key_seg = segments_of(key_pos, limits)
    allowed = key_mask(query_pos, query_seg, key_pos, key_seg)
    keys_four = key_piece.reshape(seqs_here, count, KV_HEADS, HEAD_DIM)
    values_four = value_piece.reshape(seqs_here, count, KV_HEADS, HEAD_DIM)
    scores = (
        jnp.einsum("stgrd,skgd->stgrk", query_rows, keys_four, preferred_element_type=jnp.float32)
        * score_scale
    )
    new_max = jnp.maximum(run_max, jnp.max(jnp.where(allowed, scores, NEG_LARGE), axis=-1))
    weights_exp = jnp.where(allowed, jnp.exp(scores - new_max[..., None]), 0.0)
    run_sum = jnp.sum(weights_exp, axis=-1)
    run_acc = jnp.einsum(
        "stgrk,skgd->stgrd",
        weights_exp.astype(jnp.bfloat16),
        values_four,
        preferred_element_type=jnp.float32,
    )
    return (new_max, run_sum, run_acc)


def general_shards(
    inputs,
    bounds,
    span_order,
    attn_gain,
    w_query,
    w_key,
    w_value,
    w_out,
    ffn_gain,
    w_gate,
    w_up,
    w_down,
    cotangent,
):
    seq_local = inputs.shape[0]
    rows = inputs.shape[1]
    width = inputs.shape[2]
    kv_width = KV_HEADS * HEAD_DIM
    group = HEADS // KV_HEADS
    block_len = rows // 2
    micro_seqs = seq_local // MICRO
    ctx_index = lax.axis_index("ctx")
    score_scale = HEAD_DIM ** (-0.5)
    my_start = ctx_index * rows
    positions = positions_of(my_start, rows, span_order, block_len)
    cosine, sine = rotary_tables(positions)

    def fetch():
        columns = (
            lax.all_gather(w_query, "ctx", axis=1, tiled=True),
            lax.all_gather(w_key, "ctx", axis=1, tiled=True),
            lax.all_gather(w_value, "ctx", axis=1, tiled=True),
            lax.all_gather(w_out, "ctx", axis=1, tiled=True),
            lax.all_gather(w_gate, "ctx", axis=1, tiled=True),
            lax.all_gather(w_up, "ctx", axis=1, tiled=True),
            lax.all_gather(w_down, "ctx", axis=1, tiled=True),
        )
        return (
            lax.all_gather(columns[0], "dp", axis=0, tiled=True),
            lax.all_gather(columns[1], "dp", axis=0, tiled=True),
            lax.all_gather(columns[2], "dp", axis=0, tiled=True),
            lax.all_gather(columns[3], "dp", axis=0, tiled=True),
            lax.all_gather(columns[4], "dp", axis=0, tiled=True),
            lax.all_gather(columns[5], "dp", axis=0, tiled=True),
            lax.all_gather(columns[6], "dp", axis=0, tiled=True),
            lax.all_gather(attn_gain, "dp", axis=0, tiled=True),
            lax.all_gather(ffn_gain, "dp", axis=0, tiled=True),
        )

    tot_query = jnp.zeros((width, width), jnp.float32)
    tot_key = jnp.zeros((width, kv_width), jnp.float32)
    tot_value = jnp.zeros((width, kv_width), jnp.float32)
    tot_out = jnp.zeros((width, width), jnp.float32)
    tot_gate = jnp.zeros((width, FF), jnp.float32)
    tot_up = jnp.zeros((width, FF), jnp.float32)
    tot_down = jnp.zeros((FF, width), jnp.float32)
    attention_gain_gradient_total = jnp.zeros((width,), jnp.float32)
    feedforward_gain_gradient_total = jnp.zeros((width,), jnp.float32)
    outputs_list = []
    grads_list = []
    for micro in range(MICRO):
        weights = fetch()
        mat_query, mat_key, mat_value, mat_out, mat_gate, mat_up, mat_down = weights[:7]
        attention_norm_gain = weights[7].astype(jnp.float32)
        feedforward_norm_gain = weights[8].astype(jnp.float32)
        first_seq = micro * micro_seqs
        token_embeddings = inputs[first_seq : first_seq + micro_seqs].astype(jnp.float32)
        limits = bounds[first_seq : first_seq + micro_seqs]
        query_seg = segments_of(positions, limits)
        attention_unit_rows, attention_inverse_root = root_mean_square_pieces(token_embeddings)
        attention_normed_input = (attention_unit_rows * attention_norm_gain).astype(jnp.bfloat16)
        query_pre = jnp.dot(attention_normed_input, mat_query, preferred_element_type=jnp.float32)
        key_pre = jnp.dot(attention_normed_input, mat_key, preferred_element_type=jnp.float32)
        value_rows = jnp.dot(
            attention_normed_input, mat_value, preferred_element_type=jnp.float32
        ).astype(jnp.bfloat16)
        query_rows = rotate(
            query_pre.reshape(micro_seqs, rows, HEADS, HEAD_DIM), cosine, sine
        ).astype(jnp.bfloat16)
        query_rows = query_rows.reshape(micro_seqs, rows, KV_HEADS, group, HEAD_DIM)
        key_rows = rotate(
            key_pre.reshape(micro_seqs, rows, KV_HEADS, HEAD_DIM), cosine, sine
        ).astype(jnp.bfloat16)
        key_rows = key_rows.reshape(micro_seqs, rows, kv_width)
        init_state = (
            jnp.full((micro_seqs, rows, KV_HEADS, group), NEG_LARGE, jnp.float32),
            jnp.zeros((micro_seqs, rows, KV_HEADS, group), jnp.float32),
            jnp.zeros((micro_seqs, rows, KV_HEADS, group, HEAD_DIM), jnp.float32),
        )
        run_max, run_sum, run_acc = attend_piece(
            init_state,
            (
                lax.all_gather(key_rows, "ctx", axis=1, tiled=True),
                lax.all_gather(value_rows, "ctx", axis=1, tiled=True),
            ),
            jnp.int32(0),
            query_rows,
            positions,
            query_seg,
            limits,
            span_order,
            block_len,
            score_scale,
        )
        mixture = run_acc / run_sum[..., None]
        log_total = run_max + jnp.log(run_sum)
        mixture_low = mixture.reshape(micro_seqs, rows, width).astype(jnp.bfloat16)
        hidden_residual = token_embeddings + jnp.dot(
            mixture_low, mat_out, preferred_element_type=jnp.float32
        )
        feedforward_unit_rows, feedforward_inverse_root = root_mean_square_pieces(hidden_residual)
        feedforward_normed_input = (feedforward_unit_rows * feedforward_norm_gain).astype(
            jnp.bfloat16
        )
        gate_value = jnp.dot(feedforward_normed_input, mat_gate, preferred_element_type=jnp.float32)
        up_value = jnp.dot(feedforward_normed_input, mat_up, preferred_element_type=jnp.float32)
        sigmoid_gate = jax.nn.sigmoid(gate_value)
        silu_gate = gate_value * sigmoid_gate
        inner_act = (silu_gate * up_value).astype(jnp.bfloat16)
        result = hidden_residual + jnp.dot(inner_act, mat_down, preferred_element_type=jnp.float32)
        outputs_list.append(result.astype(jnp.bfloat16))
        weights = fetch()
        mat_query, mat_key, mat_value, mat_out, mat_gate, mat_up, mat_down = weights[:7]
        output_gradient_float = cotangent[first_seq : first_seq + micro_seqs].astype(jnp.float32)
        grad_ffn_low = output_gradient_float.astype(jnp.bfloat16)
        tot_down = tot_down + jnp.einsum(
            "stf,std->fd", inner_act, grad_ffn_low, preferred_element_type=jnp.float32
        )
        grad_inner = jnp.einsum(
            "std,fd->stf", grad_ffn_low, mat_down, preferred_element_type=jnp.float32
        )
        grad_gate = (
            grad_inner * up_value * sigmoid_gate * (1.0 + gate_value * (1.0 - sigmoid_gate))
        ).astype(jnp.bfloat16)
        grad_up = (grad_inner * silu_gate).astype(jnp.bfloat16)
        tot_gate = tot_gate + jnp.einsum(
            "ste,stf->ef", feedforward_normed_input, grad_gate, preferred_element_type=jnp.float32
        )
        tot_up = tot_up + jnp.einsum(
            "ste,stf->ef", feedforward_normed_input, grad_up, preferred_element_type=jnp.float32
        )
        feedforward_normed_gradient = jnp.einsum(
            "stf,ef->ste", grad_gate, mat_gate, preferred_element_type=jnp.float32
        ) + jnp.einsum("stf,ef->ste", grad_up, mat_up, preferred_element_type=jnp.float32)
        feedforward_gain_gradient_total = feedforward_gain_gradient_total + jnp.sum(
            feedforward_normed_gradient * feedforward_unit_rows, axis=(0, 1)
        )
        hidden_state_gradient = output_gradient_float + root_mean_square_backward(
            feedforward_normed_gradient * feedforward_norm_gain,
            feedforward_unit_rows,
            feedforward_inverse_root,
        )
        grad_attn_low = hidden_state_gradient.astype(jnp.bfloat16)
        tot_out = tot_out + jnp.einsum(
            "std,ste->de", mixture_low, grad_attn_low, preferred_element_type=jnp.float32
        )
        grad_mix_low = jnp.einsum(
            "ste,de->std", grad_attn_low, mat_out, preferred_element_type=jnp.float32
        ).astype(jnp.bfloat16)
        grad_mix_five = grad_mix_low.reshape(micro_seqs, rows, KV_HEADS, group, HEAD_DIM)
        delta_rows = jnp.sum(grad_mix_five.astype(jnp.float32) * mixture, axis=-1)

        def back_piece(key_piece, value_piece, start):
            key_pos = positions_of(start, rows, span_order, block_len)
            key_seg = segments_of(key_pos, limits)
            allowed = key_mask(positions, query_seg, key_pos, key_seg)
            keys_four = key_piece.reshape(micro_seqs, rows, KV_HEADS, HEAD_DIM)
            values_four = value_piece.reshape(micro_seqs, rows, KV_HEADS, HEAD_DIM)
            scores = (
                jnp.einsum(
                    "stgrd,skgd->stgrk", query_rows, keys_four, preferred_element_type=jnp.float32
                )
                * score_scale
            )
            probs = jnp.where(allowed, jnp.exp(scores - log_total[..., None]), 0.0)
            grad_prob = jnp.einsum(
                "stgrd,skgd->stgrk", grad_mix_five, values_four, preferred_element_type=jnp.float32
            )
            grad_score = (probs * (grad_prob - delta_rows[..., None])).astype(jnp.bfloat16)
            query_term = jnp.einsum(
                "stgrk,skgd->stgrd", grad_score, keys_four, preferred_element_type=jnp.float32
            )
            key_term = jnp.einsum(
                "stgrk,stgrd->skgd", grad_score, query_rows, preferred_element_type=jnp.float32
            )
            value_term = jnp.einsum(
                "stgrk,stgrd->skgd",
                probs.astype(jnp.bfloat16),
                grad_mix_five,
                preferred_element_type=jnp.float32,
            )
            return (
                query_term,
                key_term.reshape(micro_seqs, rows, kv_width),
                value_term.reshape(micro_seqs, rows, kv_width),
            )

        query_zero = jnp.zeros((micro_seqs, rows, KV_HEADS, group, HEAD_DIM), jnp.float32)
        key_source = (
            lax.all_gather(key_rows, "ctx", axis=1, tiled=True),
            lax.all_gather(value_rows, "ctx", axis=1, tiled=True),
        )
        source_keys, source_values = key_source
        full_len = source_keys.shape[1]

        def backward_step(position_index, state):
            grad_query, key_sums, value_sums = state
            start = position_index * rows
            key_piece = lax.dynamic_slice_in_dim(source_keys, start, rows, 1)
            value_piece = lax.dynamic_slice_in_dim(source_values, start, rows, 1)
            query_term, key_term, value_term = back_piece(key_piece, value_piece, start)
            key_sums = lax.dynamic_update_slice_in_dim(key_sums, key_term, start, 1)
            value_sums = lax.dynamic_update_slice_in_dim(value_sums, value_term, start, 1)
            return (grad_query + query_term, key_sums, value_sums)

        back_init = (
            query_zero,
            jnp.zeros((micro_seqs, full_len, kv_width), jnp.float32),
            jnp.zeros((micro_seqs, full_len, kv_width), jnp.float32),
        )
        grad_query, key_sums, value_sums = lax.fori_loop(
            0, full_len // rows, backward_step, back_init
        )
        key_mine, value_mine = (
            lax.psum_scatter(
                key_sums.astype(jnp.bfloat16), "ctx", scatter_dimension=1, tiled=True
            ).astype(jnp.float32),
            lax.psum_scatter(
                value_sums.astype(jnp.bfloat16), "ctx", scatter_dimension=1, tiled=True
            ).astype(jnp.float32),
        )
        grad_q_low = rotate_back(
            (grad_query * score_scale).reshape(micro_seqs, rows, HEADS, HEAD_DIM), cosine, sine
        )
        grad_q_low = grad_q_low.reshape(micro_seqs, rows, width).astype(jnp.bfloat16)
        grad_k_low = rotate_back(
            (key_mine * score_scale).reshape(micro_seqs, rows, KV_HEADS, HEAD_DIM), cosine, sine
        )
        grad_k_low = grad_k_low.reshape(micro_seqs, rows, kv_width).astype(jnp.bfloat16)
        grad_v_low = value_mine.astype(jnp.bfloat16)
        tot_query = tot_query + jnp.einsum(
            "ste,std->ed", attention_normed_input, grad_q_low, preferred_element_type=jnp.float32
        )
        tot_key = tot_key + jnp.einsum(
            "ste,std->ed", attention_normed_input, grad_k_low, preferred_element_type=jnp.float32
        )
        tot_value = tot_value + jnp.einsum(
            "ste,std->ed", attention_normed_input, grad_v_low, preferred_element_type=jnp.float32
        )
        attention_normed_gradient = (
            jnp.einsum("std,ed->ste", grad_q_low, mat_query, preferred_element_type=jnp.float32)
            + jnp.einsum("std,ed->ste", grad_k_low, mat_key, preferred_element_type=jnp.float32)
            + jnp.einsum("std,ed->ste", grad_v_low, mat_value, preferred_element_type=jnp.float32)
        )
        attention_gain_gradient_total = attention_gain_gradient_total + jnp.sum(
            attention_normed_gradient * attention_unit_rows, axis=(0, 1)
        )
        layer_input_gradient = hidden_state_gradient + root_mean_square_backward(
            attention_normed_gradient * attention_norm_gain,
            attention_unit_rows,
            attention_inverse_root,
        )
        grads_list.append(layer_input_gradient.astype(jnp.bfloat16))
    row_sums = (
        lax.psum_scatter(
            tot_query.astype(jnp.bfloat16), "dp", scatter_dimension=0, tiled=True
        ).astype(jnp.float32),
        lax.psum_scatter(
            tot_key.astype(jnp.bfloat16), "dp", scatter_dimension=0, tiled=True
        ).astype(jnp.float32),
        lax.psum_scatter(
            tot_value.astype(jnp.bfloat16), "dp", scatter_dimension=0, tiled=True
        ).astype(jnp.float32),
        lax.psum_scatter(
            tot_out.astype(jnp.bfloat16), "dp", scatter_dimension=0, tiled=True
        ).astype(jnp.float32),
        lax.psum_scatter(
            tot_gate.astype(jnp.bfloat16), "dp", scatter_dimension=0, tiled=True
        ).astype(jnp.float32),
        lax.psum_scatter(tot_up.astype(jnp.bfloat16), "dp", scatter_dimension=0, tiled=True).astype(
            jnp.float32
        ),
        lax.psum_scatter(
            tot_down.astype(jnp.bfloat16), "dp", scatter_dimension=0, tiled=True
        ).astype(jnp.float32),
        lax.psum_scatter(
            attention_gain_gradient_total.astype(jnp.bfloat16),
            "dp",
            scatter_dimension=0,
            tiled=True,
        ).astype(jnp.float32),
        lax.psum_scatter(
            feedforward_gain_gradient_total.astype(jnp.bfloat16),
            "dp",
            scatter_dimension=0,
            tiled=True,
        ).astype(jnp.float32),
    )
    col_sums = (
        lax.psum_scatter(
            row_sums[0].astype(jnp.bfloat16), "ctx", scatter_dimension=1, tiled=True
        ).astype(jnp.float32),
        lax.psum_scatter(
            row_sums[1].astype(jnp.bfloat16), "ctx", scatter_dimension=1, tiled=True
        ).astype(jnp.float32),
        lax.psum_scatter(
            row_sums[2].astype(jnp.bfloat16), "ctx", scatter_dimension=1, tiled=True
        ).astype(jnp.float32),
        lax.psum_scatter(
            row_sums[3].astype(jnp.bfloat16), "ctx", scatter_dimension=1, tiled=True
        ).astype(jnp.float32),
        lax.psum_scatter(
            row_sums[4].astype(jnp.bfloat16), "ctx", scatter_dimension=1, tiled=True
        ).astype(jnp.float32),
        lax.psum_scatter(
            row_sums[5].astype(jnp.bfloat16), "ctx", scatter_dimension=1, tiled=True
        ).astype(jnp.float32),
        lax.psum_scatter(
            row_sums[6].astype(jnp.bfloat16), "ctx", scatter_dimension=1, tiled=True
        ).astype(jnp.float32),
    )
    gain_totals = lax.psum((row_sums[7], row_sums[8]), "ctx")
    return (
        jnp.concatenate(outputs_list, axis=0),
        jnp.concatenate(grads_list, axis=0),
        gain_totals[0],
        col_sums[0],
        col_sums[1],
        col_sums[2],
        col_sums[3],
        gain_totals[1],
        col_sums[4],
        col_sums[5],
        col_sums[6],
    )


BF = jnp.bfloat16
F32 = jnp.float32
FR = 256
FC = 512
LOG2E = 1.4426950408889634
NN = (((1,), (0,)), ((), ()))
NT = (((1,), (1,)), ((), ()))
TN = (((0,), (0,)), ((), ()))


def dot(a, b, dims=NN):
    return lax.dot_general(a, b, dims, preferred_element_type=F32)


def call(body, outs, scratch, args, vmem, name):
    specs = [pl.BlockSpec(memory_space=pltpu.SMEM)] + [
        pl.BlockSpec(memory_space=pltpu.VMEM) for _ in args[1:]
    ]
    return pl.pallas_call(
        body,
        out_shape=outs,
        in_specs=specs,
        out_specs=[pl.BlockSpec(memory_space=pltpu.VMEM) for _ in outs],
        scratch_shapes=scratch,
        compiler_params=pltpu.CompilerParams(vmem_limit_bytes=vmem * 1024 * 1024),
        cost_estimate=pl.CostEstimate(flops=1000000, bytes_accessed=1000000, transcendentals=0),
        name=name,
    )(*args)


def shape(dims, dtype):
    return jax.ShapeDtypeStruct(dims, dtype)


def spans_in(dest, blocks):
    for r in range(4):
        dest[2 * r] = blocks[r][:, :128]
        dest[2 * r + 1] = blocks[r][:, 128:]


def span_rows(info, ref, p):
    return jnp.transpose(ref[info[p]].astype(F32))


def spans_out(scr, outs):
    for r, out in enumerate(outs):
        out[:, :128] = scr[2 * r]
        out[:, 128:] = scr[2 * r + 1]


def rotary_swap(v):
    lane = lax.broadcasted_iota(jnp.int32, v.shape, 1)
    return jnp.where(lane % 64 < 32, pltpu.roll(v, 96, 1), pltpu.roll(v, 32, 1))


def qkv_body(info, x_all, x1, x2, x3, *rest):
    pieces = rest[:2]
    cos_ref, sin_ref = rest[2:4]
    q_out, k_out, v_out = rest[4:7], rest[7:10], rest[10:13]
    xp_out, wqk_out, wv_out, gain_out, raw, w32 = rest[13:]
    c, z, core = info[8], info[9], info[10]
    spans_in(raw, [x_all[c], x1[...], x2[...], x3[...]])
    for p in range(8):
        xp_out[128 * p : 128 * p + 128, :] = span_rows(info, raw, p).astype(BF)
    for j in range(2):
        for k in range(4):
            row = (lax.rem(z - k + 4, 4) * 2 + (core ^ j)) * 72
            row = pl.multiple_of(row, 8)
            for cc in range(4):
                w32[pl.ds(row, 72), 256 * cc : 256 * cc + 256] = pieces[j][c ^ cc, k].astype(F32)
    wq = [w32[:, 256 * cc : 256 * cc + 144] for cc in range(4)]
    wk = [w32[:, 256 * cc + 144 : 256 * cc + 192] for cc in range(4)]
    wv = [w32[:, 256 * cc + 192 : 256 * cc + 240] for cc in range(4)]
    wqk_out[...] = jnp.concatenate(wq + wk, axis=1).astype(BF)
    wv_out[...] = jnp.concatenate(wv, axis=1).astype(BF)
    gains = jnp.transpose(w32[:, 128:256])
    gain_out[...] = gains[112:120, :]
    g1 = gains[112:113, :]
    for i in range(4):
        rows = pl.ds(256 * i, 256)
        x = xp_out[rows, :].astype(F32)
        inv = lax.rsqrt(jnp.mean(x * x, axis=-1, keepdims=True) + EPSILON)
        n = (x * inv * g1).astype(BF)
        qk = dot(n, wqk_out[...])
        v = dot(n, wv_out[...])
        cs, sn = cos_ref[rows, :], sin_ref[rows, :]
        for b in range(6):
            t = qk[:, 128 * b : 128 * b + 128]
            t = (t * cs + rotary_swap(t) * sn).astype(BF)
            for u in range(2):
                h = 2 * b + u
                part = t[:, 64 * u : 64 * u + 64]
                if h < 9:
                    q_out[h // 3][i, 256 * (h % 3) : 256 * (h % 3) + 256, :] = part
                else:
                    k_out[h - 9][rows, :] = part
        v = v.astype(BF)
        for g in range(3):
            v_out[g][rows, :] = v[:, 64 * g : 64 * g + 64]


def segment_start(info, pos):
    b0, b1 = info[11], info[12]
    return jnp.where(pos >= b1, b1, jnp.where(pos >= b0, b0, 0))


def attend_body(info, q_ref, k_ref, v_ref, mix_out, lse_out):
    scale = 0.125 * LOG2E
    for i in range(4):
        kpos = lax.broadcasted_iota(jnp.int32, (256, 256), 1)
        qpos = lax.broadcasted_iota(jnp.int32, (256, 256), 0) + 256 * i
        first = segment_start(info, qpos)
        parts = []
        for r in range(3):
            q = q_ref[i, 256 * r : 256 * r + 256, :]
            tiles = []
            top = None
            for j in range(i + 1):
                s = dot(q, k_ref[256 * j : 256 * j + 256, :], NT) * scale
                ok = None
                if j == 0 or i == 3:
                    ok = (kpos + 256 * j) >= first
                if j == i:
                    causal = (kpos + 256 * j) <= qpos
                    ok = causal if ok is None else ok & causal
                if ok is not None:
                    s = jnp.where(ok, s, NEG_LARGE)
                tiles.append(s)
                m = jnp.maximum(s[:, :128], s[:, 128:])
                top = m if top is None else jnp.maximum(top, m)
            m = jnp.max(top, axis=-1, keepdims=True)
            total = None
            acc = None
            for j in range(i + 1):
                e = jnp.exp2(tiles[j] - m)
                part = e[:, :128] + e[:, 128:]
                total = part if total is None else total + part
                o = dot(e.astype(BF), v_ref[256 * j : 256 * j + 256, :])
                acc = o if acc is None else acc + o
            total = jnp.sum(total, axis=-1, keepdims=True)
            parts.append((acc / total).astype(BF))
            lse = m + jnp.log2(total)
            lse_out[r, :, 256 * i : 256 * i + 256] = jnp.transpose(jnp.broadcast_to(lse, (256, 128)))[0:8, :]
        mix_out[256 * i : 256 * i + 256, :] = jnp.concatenate(parts, axis=1)


def ffn_body(info, xp, m0, m1, m2, gains, *rest):
    groups = rest[:6]
    d_all, d1, d2, d3 = rest[6:10]
    y0, y1, y2, y3, dhid_out, dmix_out, delta_out, gm_out, go_out = rest[10:19]
    w32, o32, wg, wu, wd, wo, raw, normed, inner, dgate, dup, yscr, dattn, gsum, mix = rest[19:]

    def piece(j, r, k):
        a, b, last = groups[3 * j : 3 * j + 3]
        at = (0, 0, 1, 1)[k]
        if r < 3:
            return (a if k in (0, 3) else b), 2 * r + at
        return (b, 6 + at) if k in (0, 3) else (last, at)

    mix[...] = jnp.concatenate([m0[...], m1[...], m2[...]], axis=1)
    c, z, core = info[8], info[9], info[10]

    def collect(lane):
        for j in range(2):
            for r in range(4):
                col = pl.multiple_of(384 * (c ^ r), 128)
                for k in range(4):
                    zz = lax.rem(z - k + 4, 4)
                    row = pl.multiple_of((2 * zz + (core ^ j)) * 72, 8)
                    ref, at = piece(j, r, k)
                    w32[pl.ds(row, 72), pl.ds(col, 384)] = ref[at, :, lane : lane + 384].astype(F32)

    collect(0)
    wg[...] = w32[...].astype(BF)
    collect(384)
    wu[...] = w32[...].astype(BF)
    for r in range(4):
        for k in range(4):
            zz = lax.rem(z - k + 4, 4)
            ref, at = piece(0, r, k)
            a = ref[at, :, 768:1408].astype(F32)
            ref, at = piece(1, r, k)
            b = ref[at, :, 768:1408].astype(F32)
            dcol = pl.multiple_of(384 * zz, 128)
            lo = jnp.where(core == 0, a, b)
            hi = jnp.where(core == 0, b, a)
            for half in range(2):
                row = pl.multiple_of(144 * (c ^ r) + 72 * half, 8)
                w32[pl.ds(row, 72), pl.ds(dcol, 384)] = jnp.concatenate(
                    [lo[:, 192 * half : 192 * half + 192], hi[:, 192 * half : 192 * half + 192]], axis=1
                )
            col = pl.multiple_of(256 * (c ^ r), 128)
            o32[pl.ds(pl.multiple_of(144 * zz, 8), 72), pl.ds(col, 256)] = lo[:, 384:640]
            o32[pl.ds(pl.multiple_of(144 * zz + 72, 8), 72), pl.ds(col, 256)] = hi[:, 384:640]
    wd[...] = w32[...].astype(BF)
    wo[...] = jnp.concatenate([o32[:, 256 * cc : 256 * cc + 144] for cc in range(4)], axis=1).astype(BF)

    spans_in(raw, [d_all[c], d1[...], d2[...], d3[...]])
    g2 = gains[1:2, :]
    gsum[...] = jnp.zeros_like(gsum)

    def chunk(i):
        rows = pl.ds(pl.multiple_of(FR * i, FR), FR)
        x = xp[rows, :].astype(F32)
        m = mix[rows, :]
        hidden = x + dot(m, wo[...])
        r2 = lax.rsqrt(jnp.mean(hidden * hidden, axis=-1, keepdims=True) + EPSILON)
        hat = hidden * r2
        n = (hat * g2).astype(BF)
        normed[rows, :] = n
        dy = jnp.concatenate([span_rows(info, raw, i * (FR // 128) + u) for u in range(FR // 128)], axis=0)
        dlow = dy.astype(BF)
        res = hidden
        dn = None
        for f in range(FF // FC):
            cols = slice(FC * f, FC * f + FC)
            gate = dot(n, wg[:, cols])
            up = dot(n, wu[:, cols])
            sg = 1.0 / (1.0 + jnp.exp(-gate))
            silu = gate * sg
            act = (silu * up).astype(BF)
            inner[rows, cols] = act
            res = res + dot(act, wd[:, cols], NT)
            din = dot(dlow, wd[:, cols])
            dg = (din * up * (sg + silu * (1.0 - sg))).astype(BF)
            du = (din * silu).astype(BF)
            dgate[rows, cols] = dg
            dup[rows, cols] = du
            t = dot(dg, wg[:, cols], NT) + dot(du, wu[:, cols], NT)
            dn = t if dn is None else dn + t
        for u in range(FR // 128):
            yscr[info[i * (FR // 128) + u]] = jnp.transpose(res[128 * u : 128 * u + 128, :]).astype(BF)
        gsum[...] += jnp.sum((dn * hat).reshape(FR // 8, 8, 576), axis=0)
        e = dn * g2
        dh = dy + r2 * (e - hat * jnp.mean(e * hat, axis=-1, keepdims=True))
        dhid_out[rows, :] = dh
        da = dh.astype(BF)
        dattn[rows, :] = da
        dm = dot(da, wo[...], NT).astype(BF)
        prod = dm.astype(F32) * m.astype(F32)
        for u in range(FR // 256):
            block = i * (FR // 256) + u
            part_rows = slice(256 * u, 256 * u + 256)
            lane = lax.broadcasted_iota(jnp.int32, (256, 128), 1)
            table = jnp.zeros((256, 128), F32)
            for h in range(9):
                dmix_out[h // 3, block, 256 * (h % 3) : 256 * (h % 3) + 256, :] = dm[part_rows, 64 * h : 64 * h + 64]
                col = jnp.sum(prod[part_rows, 64 * h : 64 * h + 64], axis=-1, keepdims=True)
                table = jnp.where(lane == h, col, table)
            delta_out[block] = jnp.transpose(table)[0:16, :]
    def step(i, carry):
        chunk(i)
        return carry

    lax.fori_loop(0, 1024 // FR, step, 0)
    spans_out(yscr, (y0, y1, y2, y3))

    def deal(lane):
        for r in range(4):
            col = pl.multiple_of(384 * (c ^ r), 128)
            for k in range(4):
                zz = lax.rem(z + k, 4)
                for out, who in ((gm_out, core), (go_out, 1 - core)):
                    row = pl.multiple_of((2 * zz + who) * 72, 8)
                    out[r, k, :, lane : lane + 384] = w32[pl.ds(row, 72), pl.ds(col, 384)].astype(BF)

    w32[...] = dot(normed[...], dgate[...], TN)
    deal(0)
    w32[...] = dot(normed[...], dup[...], TN)
    deal(384)
    for p in range(8):
        normed[128 * p : 128 * p + 128, :] = span_rows(info, raw, p).astype(BF)
    w32[...] = dot(normed[...], inner[...], TN)
    og = dot(mix[...], dattn[...], TN)
    for cc in range(4):
        o32[:, 256 * cc : 256 * cc + 144] = og[:, 144 * cc : 144 * cc + 144]
    total = jnp.sum(gsum[...], axis=0, keepdims=True)
    gcol = jnp.transpose(jnp.broadcast_to(total, (128, 576)))
    for cc in range(4):
        o32[:, 256 * cc + 144 : 256 * cc + 256] = gcol[:, 0:112]
    for r in range(4):
        ocol = pl.multiple_of(256 * (c ^ r), 128)
        for k in range(4):
            zz = lax.rem(z + k, 4)
            dcol = pl.multiple_of(384 * zz, 128)
            a = w32[pl.ds(pl.multiple_of(144 * (c ^ r), 8), 72), pl.ds(dcol, 384)]
            b = w32[pl.ds(pl.multiple_of(144 * (c ^ r) + 72, 8), 72), pl.ds(dcol, 384)]
            left = [a[:, :192], b[:, :192]]
            right = [a[:, 192:], b[:, 192:]]
            for out, who in ((gm_out, core), (go_out, 1 - core)):
                row = pl.multiple_of((2 * zz + who) * 72, 8)
                o = o32[pl.ds(row, 72), pl.ds(ocol, 256)]
                d = [jnp.where(who == 0, u, v) for u, v in zip(left, right)]
                out[r, k, :, 768:1408] = jnp.concatenate(d + [o], axis=1).astype(BF)


def back_body(
    info, q_ref, k_ref, v_ref, dmix_ref, lse_ref, delta_ref, cos_ref, sin_ref, out, dq_scr, dk_scr, dv_scr, *, g
):
    scale = 0.125 * LOG2E
    dk_scr[...] = jnp.zeros_like(dk_scr)
    dv_scr[...] = jnp.zeros_like(dv_scr)
    for i in range(4):
        qpos = lax.broadcasted_iota(jnp.int32, (256, 256), 1) + 256 * i
        kpos = lax.broadcasted_iota(jnp.int32, (256, 256), 0)
        first = segment_start(info, qpos)
        for r in range(3):
            q = q_ref[i, 256 * r : 256 * r + 256, :]
            do = dmix_ref[g, i, 256 * r : 256 * r + 256, :]
            lse = lse_ref[r, 0:1, 256 * i : 256 * i + 256]
            delta = delta_ref[i, 3 * g + r : 3 * g + r + 1, :]
            dq = None
            for j in range(i + 1):
                keys = slice(256 * j, 256 * j + 256)
                kk = k_ref[keys, :]
                s = dot(kk, q, NT) * scale
                p = jnp.exp2(s - lse)
                ok = None
                if j == 0 or i == 3:
                    ok = (kpos + 256 * j) >= first
                if j == i:
                    causal = (kpos + 256 * j) <= qpos
                    ok = causal if ok is None else ok & causal
                if ok is not None:
                    p = jnp.where(ok, p, 0.0)
                dp = dot(v_ref[keys, :], do, NT)
                ds = (p * (dp - delta)).astype(BF)
                dv_scr[keys, :] += dot(p.astype(BF), do)
                dk_scr[keys, :] += dot(ds, q)
                t = dot(ds, kk, TN)
                dq = t if dq is None else dq + t
            dq_scr[r, 256 * i : 256 * i + 256, :] = dq
    for i in range(4):
        rows = slice(256 * i, 256 * i + 256)
        cs, sn = cos_ref[rows, :], sin_ref[rows, :]
        done = []
        for pair in ((dq_scr[0, rows, :], dq_scr[1, rows, :]), (dq_scr[2, rows, :], dk_scr[rows, :])):
            t = jnp.concatenate(pair, axis=1) * 0.125
            done.append((t * cs - rotary_swap(t) * sn).astype(BF))
        last = jnp.concatenate([dv_scr[rows, :], jnp.zeros((256, 64), F32)], axis=1).astype(BF)
        out[rows, :] = jnp.concatenate(done + [last], axis=1)


def joined(parts):
    qk = jnp.concatenate([d[:, 0:192] for d in parts] + [d[:, 192:256] for d in parts], axis=1)
    return qk, jnp.concatenate([d[:, 256:320] for d in parts], axis=1)


def project_grad_body(
    info, xp, d0, d1, d2, dhid, wqk, wv, gains, i0, i1, i2, i3, gm_out, go_out, n_scr, gsum, w32, yscr
):
    c, z, core = info[8], info[9], info[10]
    g1 = gains[0:1, :]
    gsum[...] = jnp.zeros_like(gsum)
    qk, vv = joined((d0, d1, d2))
    for i in range(4):
        rows = slice(256 * i, 256 * i + 256)
        x = xp[rows, :].astype(F32)
        r1 = lax.rsqrt(jnp.mean(x * x, axis=-1, keepdims=True) + EPSILON)
        hat = x * r1
        n_scr[rows, :] = (hat * g1).astype(BF)
        dn = dot(qk[rows, :], wqk[...], NT) + dot(vv[rows, :], wv[...], NT)
        gsum[...] += jnp.sum((dn * hat).reshape(32, 8, 576), axis=0)
        e = dn * g1
        res = dhid[rows, :] + r1 * (e - hat * jnp.mean(e * hat, axis=-1, keepdims=True))
        for u in range(2):
            yscr[info[2 * i + u]] = jnp.transpose(res[128 * u : 128 * u + 128, :]).astype(BF)
    spans_out(yscr, (i0, i1, i2, i3))
    gqk = dot(n_scr[...], qk, TN)
    gv = dot(n_scr[...], vv, TN)
    total = jnp.sum(gsum[...], axis=0, keepdims=True)
    gcol = jnp.transpose(jnp.broadcast_to(total, (128, 576)))
    for cc in range(4):
        w32[:, 256 * cc : 256 * cc + 256] = jnp.concatenate(
            [
                gqk[:, 144 * cc : 144 * cc + 144],
                gqk[:, 576 + 48 * cc : 576 + 48 * cc + 48],
                gv[:, 48 * cc : 48 * cc + 48],
                gcol[:, 0:16],
            ],
            axis=1,
        )
    for r in range(4):
        col = pl.multiple_of(256 * (c ^ r), 128)
        for k in range(4):
            zz = lax.rem(z + k, 4)
            for out, who in ((gm_out, core), (go_out, 1 - core)):
                row = pl.multiple_of((2 * zz + who) * 72, 8)
                out[r, k] = w32[pl.ds(row, 72), pl.ds(col, 256)].astype(BF)


def last_body(info, q, k, v, dmix, lse, delta, cos, sin, xp, d0, d1, dhid, wqk, wv, gains, *rest):
    i0, i1, i2, i3, gm_out, go_out = rest[:6]
    d2, dq_scr, dk_scr, dv_scr, n_scr, gsum, w32, yscr = rest[6:]
    back_body(info, q, k, v, dmix, lse, delta, cos, sin, d2, dq_scr, dk_scr, dv_scr, g=2)
    project_grad_body(
        info, xp, d0, d1, d2, dhid, wqk, wv, gains, i0, i1, i2, i3, gm_out, go_out, n_scr, gsum, w32, yscr
    )


def place_body(info, a, b, c_, d, out):
    for r, ref in enumerate((a, b, c_, d)):
        out[info[8] ^ r] = ref[...]


def pack_body(q, kt, vt, a, f, out):
    out[:, 0:144] = q[...]
    out[:, 144:256] = jnp.concatenate(
        [
            jnp.transpose(kt[...].astype(F32)),
            jnp.transpose(vt[...].astype(F32)),
            jnp.transpose(jnp.concatenate([a[...].astype(F32), f[...].astype(F32), jnp.zeros((14, 72), F32)], axis=0)),
        ],
        axis=1,
    ).astype(BF)


def first_finish_body(a, b, c_, d, gain, query, key_t, value_t):
    total = a[...].astype(F32) + b[...].astype(F32) + c_[...].astype(F32) + d[...].astype(F32)
    query[...] = total[:, 0:144]
    rest = jnp.transpose(total[:, 128:256])
    key_t[...] = rest[16:64]
    value_t[...] = rest[64:112]
    gain[...] = rest[112:113]


def second_finish_body(a, b, c_, d, gate, up, down_t, out, gain):
    total = a[...].astype(F32) + b[...].astype(F32) + c_[...].astype(F32) + d[...].astype(F32)
    gate[...] = total[:, 0:384]
    up[...] = total[:, 384:768]
    down_t[0:72, :] = total[:, 768:960]
    down_t[72:144, :] = total[:, 960:1152]
    out[...] = total[:, 1152:1296]
    gain[...] = jnp.transpose(total[:, 1280:1408])[16:17]


CORE_SWAP = [(i, i ^ 1) for i in range(8)]


def z_shift(v, k):
    return lax.ppermute(v, "dp", [(i, (i + 2 * k) % 8) for i in range(8)])


def plane_swap(v, k):
    return lax.ppermute(v, "ctx", [(i, i ^ k) for i in range(4)])


def core_swap(v):
    return lax.ppermute(v, "dp", CORE_SWAP)


def add_up(parts):
    total = parts[0].astype(F32)
    for part in parts[1:]:
        total = total + part.astype(F32)
    return total


def fast_shards(
    inputs,
    bounds,
    span_order,
    attn_gain,
    w_query,
    w_key,
    w_value,
    w_out,
    ffn_gain,
    w_gate,
    w_up,
    w_down,
    cotangent,
):
    c = lax.axis_index("ctx").astype(jnp.int32)
    dp = lax.axis_index("dp").astype(jnp.int32)
    slots = jnp.sum(
        jnp.where(
            span_order[None, :] == jnp.arange(8, dtype=jnp.int32)[:, None],
            jnp.arange(8, dtype=jnp.int32)[None, :],
            0,
        ),
        axis=1,
    )
    blocks = ((slots // 2) ^ c) * 2 + slots % 2
    limits = lax.dynamic_index_in_dim(bounds, c, 0, keepdims=False)
    info = jnp.concatenate([blocks, jnp.stack([c, dp // 2, dp % 2]), limits, jnp.zeros((3,), jnp.int32)])

    def after(value, *first):
        return lax.optimization_barrier((value, *first))[0]

    x_rows = jnp.swapaxes(inputs, 1, 2)
    d_rows = jnp.swapaxes(cotangent, 1, 2)

    def exchange(rows, k):
        return plane_swap(lax.dynamic_index_in_dim(rows, c ^ k, 0, keepdims=False), k)

    pack1 = pl.pallas_call(pack_body, out_shape=shape((72, 256), BF), name="pack")(
        w_query, w_key.T, w_value.T, attn_gain[None, :], ffn_gain[None, :]
    )
    line1 = [pack1] + [z_shift(pack1, k) for k in (1, 2, 3)]
    x1, x2 = exchange(x_rows, 1), exchange(x_rows, 2)
    flat1 = jnp.stack(line1)
    near = [flat1] + [plane_swap(flat1, k) for k in (1, 2, 3)]
    gate_late, down_t = lax.optimization_barrier((w_gate, w_down.T, flat1))[:2]
    pack2 = jnp.concatenate(
        [gate_late, w_up, down_t[:72], down_t[72:], w_out, jnp.zeros((72, 112), BF)], axis=1
    )
    x3 = exchange(after(x_rows, x1, x2), 3)
    near_all = jnp.stack(near)
    pack2_later = after(pack2, near_all)
    z_three = z_shift(pack2_later, 3)
    far_all = core_swap(near_all)
    pack2_last = after(pack2, far_all)
    z_one, z_two = z_shift(pack2_last, 1), z_shift(pack2_last, 2)
    z_three, x3, far_all = lax.optimization_barrier((z_three, x3, far_all))
    line_a = jnp.stack([pack2, z_three])
    a_x, a_y = plane_swap(line_a, 1), plane_swap(line_a, 2)

    positions = after(jnp.arange(1024, dtype=jnp.int32), *near)
    half = HEAD_DIM // 2
    frequency = THETA ** (-jnp.arange(half).astype(F32) / half)
    angles = positions.astype(F32)[:, None] * frequency[None, :]
    cosine, sine = jnp.cos(angles), jnp.sin(angles)
    cos4 = jnp.concatenate([cosine] * 4, axis=1)
    sin4 = jnp.concatenate([-sine, sine, -sine, sine], axis=1)

    made = call(
        qkv_body,
        [shape((4, 768, 64), BF)] * 3
        + [shape((1024, 64), BF)] * 6
        + [
            shape((1024, 576), BF),
            shape((576, 768), BF),
            shape((576, 192), BF),
            shape((8, 576), F32),
        ],
        [pltpu.VMEM((8, 576, 128), BF), pltpu.VMEM((576, 1024), F32)],
        [info, after(x_rows, line_a), x1, x2, x3, near_all, far_all, cos4, sin4],
        40,
        "project",
    )
    q, k, v = made[0:3], made[3:6], made[6:9]
    xp, wqk, wv, gains = made[9:]
    def attend(g, q_):
        return call(
            attend_body,
            [shape((1024, 192), BF), shape((3, 8, 1024), F32)],
            [],
            [info, q_, k[g], v[g]],
            24,
            "attend",
        )

    z_one, z_two, d_first, q0 = lax.optimization_barrier((z_one, z_two, d_rows, q[0]))
    line_b = jnp.stack([z_one, z_two])
    q0 = after(q0, line_b)
    b_x, b_y = plane_swap(line_b, 1), plane_swap(line_b, 2)
    d1 = exchange(d_first, 1)
    mix0, lse0 = attend(0, q0)
    a_x, a_y, mix0, d_second = lax.optimization_barrier((a_x, a_y, mix0, d_rows))
    a_low, a_high = plane_swap(a_x[:1], 2), plane_swap(a_y[1:], 1)
    d2 = exchange(d_second, 2)
    mix1, lse1 = attend(1, after(q[1], mix0))
    b_x, b_y, d1, mix1, d_third = lax.optimization_barrier((b_x, b_y, d1, mix1, d_rows))
    b_low, b_high = plane_swap(b_x[:1], 2), plane_swap(b_y[1:], 1)
    d3 = exchange(d_third, 3)
    mix2, lse2 = attend(2, after(q[2], mix1, a_low, a_high))
    b_low, b_high, d3, mix2 = lax.optimization_barrier((b_low, b_high, d3, mix2))
    mixes, lses = [mix0, mix1, mix2], [lse0, lse1, lse2]
    own_parts = [
        jnp.concatenate([line_a, a_x, a_y], axis=0),
        jnp.concatenate([line_b, b_x, b_y, a_low, a_high], axis=0),
        jnp.concatenate([b_low, b_high], axis=0),
    ]
    pieces2 = own_parts + [core_swap(v_) for v_ in own_parts]
    d_parts = [d1, d2, d3]
    y0, y1, y2, y3, dhid, dmix, delta, gm2, go2 = call(
        ffn_body,
        [shape((576, 256), BF)] * 4
        + [
            shape((1024, 576), F32),
            shape((3, 4, 768, 64), BF),
            shape((4, 16, 256), F32),
            shape((4, 4, 72, 1408), BF),
            shape((4, 4, 72, 1408), BF),
        ],
        [
            pltpu.VMEM((576, 1536), F32),
            pltpu.VMEM((576, 1024), F32),
            pltpu.VMEM((576, 1536), BF),
            pltpu.VMEM((576, 1536), BF),
            pltpu.VMEM((576, 1536), BF),
            pltpu.VMEM((576, 576), BF),
            pltpu.VMEM((8, 576, 128), BF),
            pltpu.VMEM((1024, 576), BF),
            pltpu.VMEM((1024, 1536), BF),
            pltpu.VMEM((1024, 1536), BF),
            pltpu.VMEM((1024, 1536), BF),
            pltpu.VMEM((8, 576, 128), BF),
            pltpu.VMEM((1024, 576), BF),
            pltpu.VMEM((8, 576), F32),
            pltpu.VMEM((1024, 576), BF),
        ],
        [info, xp] + mixes + [gains] + pieces2 + [d_rows] + d_parts,
        60,
        "feedforward",
    )

    def core_sum(mine, others):
        return add_up([mine, core_swap(others)]).astype(BF)

    def place(parts):
        placed = call(place_body, [shape((4, 576, 256), BF)], [], [info] + parts, 16, "place")[0]
        return jnp.swapaxes(placed, 1, 2)

    def attend_back(g, *first):
        return call(
            functools.partial(back_body, g=g),
            [shape((1024, 384), BF)],
            [pltpu.VMEM((3, 1024, 64), F32), pltpu.VMEM((1024, 64), F32), pltpu.VMEM((1024, 64), F32)],
            [info, after(q[g], *first) if first else q[g], k[g], v[g], dmix, lses[g], delta, cos4, sin4],
            24,
            "attend_back",
        )[0]

    both = core_sum(gm2, go2)
    y1, y2 = plane_swap(y1, 1), plane_swap(y2, 2)
    grad0 = attend_back(0)
    both, grad0, y1, y2, y3 = lax.optimization_barrier((both, grad0, y1, y2, y3))
    low = plane_swap(both[3, :2], 2)
    high = plane_swap(both[3, 2:], 1)
    y3 = plane_swap(y3, 3)
    grad1 = attend_back(1, grad0, both)
    low, high, grad1, y3 = lax.optimization_barrier((low, high, grad1, y3))
    one = jnp.concatenate([add_up([both[1, :2], low]).astype(BF), both[1, 2:]], axis=0)
    two = jnp.concatenate([both[2, :2], add_up([both[2, 2:], high]).astype(BF)], axis=0)
    one_got, two_got = plane_swap(one, 1), plane_swap(two, 2)
    output = place([y0, y1, y2, y3])
    i0, i1, i2, i3, gm1, go1 = call(
        last_body,
        [shape((576, 256), BF)] * 4 + [shape((4, 4, 72, 256), BF), shape((4, 4, 72, 256), BF)],
        [
            pltpu.VMEM((1024, 384), BF),
            pltpu.VMEM((3, 1024, 64), F32),
            pltpu.VMEM((1024, 64), F32),
            pltpu.VMEM((1024, 64), F32),
            pltpu.VMEM((1024, 576), BF),
            pltpu.VMEM((8, 576), F32),
            pltpu.VMEM((576, 1024), F32),
            pltpu.VMEM((8, 576, 128), BF),
        ],
        [info, after(q[2], grad1, one, two), k[2], v[2], dmix, lses[2], delta, cos4, sin4]
        + [xp, grad0, grad1, dhid, wqk, wv, gains],
        40,
        "attend_back_input_gradient",
    )
    one_got, two_got, gm1, go1, i1, i2, i3 = lax.optimization_barrier((one_got, two_got, gm1, go1, i1, i2, i3))
    both1 = core_sum(gm1, go1)
    i1, i2 = plane_swap(i1, 1), plane_swap(i2, 2)
    total2 = add_up([both[0], one_got, two_got]).astype(BF)
    two_one, two_three = z_shift(total2[1], 1), z_shift(total2[3], 3)
    both1, i3, i1, i2, total2 = lax.optimization_barrier((both1, i3, i1, i2, total2))
    two_two = z_shift(total2[2], 2)
    first_got = [plane_swap(both1[r], r) for r in (1, 2, 3)]
    i3 = plane_swap(i3, 3)
    total1 = add_up([both1[0]] + first_got).astype(BF)
    total1, two_one, two_three = lax.optimization_barrier((total1, two_one, two_three))
    line2 = [total2[0], two_one, two_two, two_three]
    line1 = [total1[0]] + [z_shift(total1[k_], k_) for k_ in (1, 2, 3)]
    input_grad = place([i0, i1, i2, i3])
    gate_g, up_g, down_t, out_g, ffn_gain_g = pl.pallas_call(
        second_finish_body,
        out_shape=[shape((72, 384), F32)] * 2 + [shape((144, 192), F32), shape((72, 144), F32), shape((1, 72), F32)],
        name="finish_second",
    )(*line2)
    attn_gain_g, query_g, key_t, value_t = pl.pallas_call(
        first_finish_body,
        out_shape=[shape((1, 72), F32), shape((72, 144), F32), shape((48, 72), F32), shape((48, 72), F32)],
        name="finish_first",
    )(*line1)
    return (
        output,
        input_grad,
        attn_gain_g[0],
        query_g,
        key_t.T,
        value_t.T,
        out_g,
        ffn_gain_g[0],
        gate_g,
        up_g,
        down_t.T,
    )


def shards(*args):
    seqs, rows, width = args[0].shape
    fits = (seqs, rows, width) == (4, 256, 576) and args[2].shape[0] == 8
    sizes = (lax.axis_size("dp"), lax.axis_size("ctx"))
    if fits and sizes == (8, 4):
        return fast_shards(*args)
    return general_shards(*args)


def solution(mesh):
    in_specs = (
        P("dp", "ctx", None),
        P("dp", None),
        P(),
        P("dp"),
        P("dp", "ctx"),
        P("dp", "ctx"),
        P("dp", "ctx"),
        P("dp", "ctx"),
        P("dp"),
        P("dp", "ctx"),
        P("dp", "ctx"),
        P("dp", "ctx"),
        P("dp", "ctx", None),
    )
    out_specs = (
        P("dp", "ctx", None),
        P("dp", "ctx", None),
        P("dp"),
        P("dp", "ctx"),
        P("dp", "ctx"),
        P("dp", "ctx"),
        P("dp", "ctx"),
        P("dp"),
        P("dp", "ctx"),
        P("dp", "ctx"),
        P("dp", "ctx"),
    )
    return jax.shard_map(shards, mesh=mesh, in_specs=in_specs, out_specs=out_specs, check_vma=False)
```
